32 devices in a mesh: rx: 16 (over z, x, core), band: 2 (over y).
Axes of the slice: x: 2, y: 2, z: 4, core: 2. Of those that a mesh axis runs over, the one named last changes fastest.
Arguments:
- spectra: bfloat16 [2, 256, 64, 2048], P(None, 'band', None, 'rx'), may hold values from -6 to 6
- source_index: int32 [16], replicated, may hold values from 0 to 2047, as said below
Outputs:
- stack: bfloat16 [2, 256, 16, 2048], P(None, 'band', None, 'rx')
The draws below stay inside these ranges and needn't reach their ends.
Inputs may be any that keep to these rules, and one draw needn't show every extreme that they name: `source_index`: virtual source s is one of channels s * 128 to (s + 1) * 128 - 1; the first and the last channel are sources.
All inputs are finite; a program needn't handle non-finite values.
Results may differ from the reference program's by a relative error of at most 0.0059.
Values may be sent and summed in bfloat16 or wider, within the bound.
No kernel may reach another device: no remote copies, remote signals or barrier semaphores. Data moves between devices by JAX's collectives and lax.ppermute only.
A program may use at most 64 MiB of HBM per device.

```python
import jax
import jax.numpy as jnp
from jax import lax

CH_DEV = 128
WINDOWS = 64
FREQS = 256
HALF = 4
SOURCES = 16
CHANNELS = 2048


def draw_source_index(key, part):
    offsets = jax.random.randint(key, (SOURCES,), 0, CH_DEV, dtype=jnp.int32)
    positions = jnp.arange(SOURCES, dtype=jnp.int32)
    offsets = jnp.where(positions == 0, 0, offsets)
    offsets = jnp.where(positions == SOURCES - 1, CH_DEV - 1, offsets)
    return (positions * CH_DEV + offsets).astype(jnp.int32)


def levels(own_key, extent, pieces, least, largest):
    factor_of = 1.0
    for dim, shards_of in pieces:
        heights = jax.random.uniform(jax.random.fold_in(jax.random.fold_in(own_key, 6), dim), (shards_of,), jnp.float32, least / len(pieces), largest / len(pieces))
        factor_of = factor_of * jnp.repeat(jnp.exp(heights), extent[dim] // shards_of).reshape((-1,) + (1,) * (len(extent) - 1 - dim))
    return factor_of


def scatter_about(own_key, dims, spread, reach, shards=(), kind=jnp.bfloat16):
    entries = jax.random.normal(own_key, dims, jnp.float32) * spread
    if len(shards) > 0:
        entries = levels(own_key, dims, shards, -0.22, 0.18) * entries
    return jnp.clip(entries, min=-reach, max=reach).astype(kind)


def setup_inputs(seed: int = 0) -> dict:
    seeds = jax.random.split(jax.random.key(seed), 3)
    return {
        "spectra": scatter_about(seeds[0], (2, FREQS, WINDOWS, CHANNELS), 1.0, 6.0, ((1, 2), (3, 16))),
        "source_index": draw_source_index(jax.random.fold_in(seeds[2], 71), 0),
    }


def reference(spectra, source_index):
    values = spectra.astype(jnp.float32)
    rounded = lax.optimization_barrier(jnp.sqrt(values[0] * values[0] + values[1] * values[1]).astype(jnp.bfloat16))
    amplitude = rounded.astype(jnp.float32)
    padded_amplitude = jnp.pad(amplitude, ((HALF, HALF), (0, 0), (0, 0)))

    def per_bin(bin_index):
        total = jnp.zeros(amplitude.shape[1:], jnp.float32)
        for offset in range(2 * HALF + 1):
            total = total + lax.dynamic_index_in_dim(padded_amplitude, bin_index + offset, 0, keepdims=False)
        smooth = total / (2 * HALF + 1)
        spectrum_bin = lax.dynamic_index_in_dim(spectra, bin_index, 1, keepdims=False).astype(jnp.float32)
        whitened = (spectrum_bin / (smooth + 0.1)[None]).astype(jnp.bfloat16)
        source_spectra = jnp.take(whitened, source_index, axis=2)
        white_real = whitened[0].astype(jnp.float32)
        white_imag = whitened[1].astype(jnp.float32)
        source_real = source_spectra[0].astype(jnp.float32)
        source_imag = source_spectra[1].astype(jnp.float32)
        real_part = jnp.einsum('wc,ws->sc', white_real, source_real) + jnp.einsum('wc,ws->sc', white_imag, source_imag)
        imag_part = jnp.einsum('wc,ws->sc', white_imag, source_real) - jnp.einsum('wc,ws->sc', white_real, source_imag)
        return (jnp.stack([real_part, imag_part], 0) / WINDOWS).astype(jnp.bfloat16)
    stacked = lax.map(per_bin, jnp.arange(FREQS, dtype=jnp.int32))
    return jnp.transpose(stacked, (1, 0, 2, 3))
```

```python
import functools

import jax
import jax.numpy as jnp
from jax import lax
from jax.experimental import pallas as pl
from jax.experimental.pallas import tpu as pltpu
from jax.sharding import PartitionSpec as P

HALF = 4
SPAN = 2 * HALF + 1
FLOOR = 0.1
PIECES = 4
TINY = 1e-37
VMEM_LIMIT = 48 * 1024 * 1024


def amplitude_of(power):
    return (power * lax.rsqrt(jnp.maximum(power, TINY))).astype(jnp.bfloat16)


def edge_amplitudes(spectra):
    count = lax.axis_size("band")
    rank = lax.axis_index("band")

    def amplitude(part):
        values = part.astype(jnp.float32)
        return jnp.sqrt(values[0] * values[0] + values[1] * values[1]).astype(jnp.bfloat16)

    first = amplitude(spectra[:, :HALF])
    last = amplitude(spectra[:, spectra.shape[1] - HALF :])
    if count == 2:
        received = lax.ppermute(jnp.where(rank == 0, last, first), "band", [(0, 1), (1, 0)])
        zero = jnp.zeros_like(received)
        return jnp.stack([jnp.where(rank == 1, received, zero), jnp.where(rank == 0, received, zero)])
    below = lax.ppermute(last, "band", [(i, i + 1) for i in range(count - 1)])
    above = lax.ppermute(first, "band", [(i + 1, i) for i in range(count - 1)])
    return jnp.stack([below, above])


def select_column(column, rows, width):
    channels = rows.shape[1]
    picks = (lax.broadcasted_iota(jnp.int32, (8, channels), 1) == column).astype(jnp.bfloat16)
    n = rows.shape[0] // width
    out = []
    for block in range(0, n, 8):
        part = rows[block * width : (block + 8) * width]
        flat = lax.dot_general(picks, part, (((1,), (1,)), ((), ())), preferred_element_type=jnp.float32)
        sublane = lax.broadcasted_iota(jnp.int32, (8, width), 0)
        total = jnp.zeros((8, width), jnp.float32)
        for k in range(8):
            total = jnp.where(sublane == k, flat[:, k * width : (k + 1) * width], total)
        out.append(total)
    return out


def extract_kernel(column_ref, spectra_ref, row_ref):
    bins, windows, channels = spectra_ref.shape[1:]
    parts = []
    for part in range(2):
        rows = spectra_ref[part].reshape(bins * windows, channels)
        parts.append(jnp.concatenate(select_column(column_ref[0], rows, windows), 0))
    row_ref[...] = jnp.concatenate(parts, 1).astype(jnp.bfloat16)


def extract_row(spectra, column):
    _, bins, windows, channels = spectra.shape
    step = min(16, bins)
    return pl.pallas_call(
        extract_kernel,
        grid=(bins // step,),
        in_specs=[
            pl.BlockSpec(memory_space=pltpu.SMEM),
            pl.BlockSpec((2, step, windows, channels), lambda i: (0, i, 0, 0)),
        ],
        out_specs=pl.BlockSpec((step, 2 * windows), lambda i: (i, 0)),
        out_shape=jax.ShapeDtypeStruct((bins, 2 * windows), jnp.bfloat16),
        compiler_params=pltpu.CompilerParams(vmem_limit_bytes=VMEM_LIMIT),
        cost_estimate=pl.CostEstimate(flops=2 * 8 * spectra.size, bytes_accessed=2 * spectra.size, transcendentals=0),
        name="extract_row",
    )(column, spectra)


def whiten_row_kernel(column_ref, row_ref, edge_ref, out_ref):
    bins, width = row_ref.shape
    windows = width // 2
    channels = edge_ref.shape[-1]
    rows = edge_ref[...].reshape(2 * HALF * windows, channels)
    edge = select_column(column_ref[0], rows, windows)[0]
    edge = jnp.concatenate([edge, edge], 1)
    values = row_ref[...].astype(jnp.float32)
    squares = values * values
    amplitude = amplitude_of(squares + pltpu.roll(squares, windows, 1))
    target = lax.broadcasted_iota(jnp.int32, (bins, bins), 0)
    source = lax.broadcasted_iota(jnp.int32, (bins, bins), 1)
    near = (jnp.abs(target - source) <= HALF).astype(jnp.bfloat16)
    target = lax.broadcasted_iota(jnp.int32, (bins, 2 * HALF), 0)
    index = lax.broadcasted_iota(jnp.int32, (bins, 2 * HALF), 1)
    source = jnp.where(index < HALF, index - HALF, index - HALF + bins)
    near_edge = (jnp.abs(target - source) <= HALF).astype(jnp.bfloat16)
    total = jnp.dot(near, amplitude, preferred_element_type=jnp.float32)
    total = total + jnp.dot(near_edge, edge.astype(jnp.bfloat16), preferred_element_type=jnp.float32)
    out_ref[...] = (values / (total / SPAN + FLOOR)).astype(jnp.bfloat16)


def whiten_row(row, edges, column):
    return pl.pallas_call(
        whiten_row_kernel,
        in_specs=[
            pl.BlockSpec(memory_space=pltpu.SMEM),
            pl.BlockSpec(memory_space=pltpu.VMEM),
            pl.BlockSpec(memory_space=pltpu.VMEM),
        ],
        out_specs=pl.BlockSpec(memory_space=pltpu.VMEM),
        out_shape=jax.ShapeDtypeStruct(row.shape, jnp.bfloat16),
        compiler_params=pltpu.CompilerParams(vmem_limit_bytes=VMEM_LIMIT),
        name="whiten_row",
    )(column, row, edges)


def whiten_kernel(spectra_ref, edge_ref, out_ref, amplitude_ref):
    bins = spectra_ref.shape[1]
    block = 16 if bins % 16 == 0 else 8
    amplitude_ref[0:HALF] = edge_ref[0].astype(jnp.float32)
    amplitude_ref[bins + HALF : bins + 2 * HALF] = edge_ref[1].astype(jnp.float32)

    @pl.loop(0, bins // block)
    def _(b):
        at = b * block
        real = spectra_ref[0, pl.ds(at, block)].astype(jnp.float32)
        imag = spectra_ref[1, pl.ds(at, block)].astype(jnp.float32)
        amplitude_ref[pl.ds(at + HALF, block)] = amplitude_of(real * real + imag * imag).astype(jnp.float32)

    @pl.loop(0, bins // block)
    def _(b):
        at = b * block
        one = [amplitude_ref[at + k] for k in range(block + 2 * HALF)]
        two = [one[k] + one[k + 1] for k in range(block + 2 * HALF - 1)]
        four = [two[k] + two[k + 2] for k in range(block + 2 * HALF - 3)]
        for k in range(block):
            total = (four[k] + four[k + 4]) + one[k + 8]
            scale = 1.0 / (total * (1.0 / SPAN) + FLOOR)
            out_ref[0, at + k] = (spectra_ref[0, at + k].astype(jnp.float32) * scale).astype(jnp.bfloat16)
            out_ref[1, at + k] = (spectra_ref[1, at + k].astype(jnp.float32) * scale).astype(jnp.bfloat16)


def whiten_piece(spectra, edges, piece):
    _, bins, windows, channels = spectra.shape
    width = windows // PIECES
    return pl.pallas_call(
        whiten_kernel,
        grid=(1,),
        in_specs=[
            pl.BlockSpec((2, bins, width, channels), lambda i: (0, 0, piece, 0)),
            pl.BlockSpec((2, HALF, width, channels), lambda i: (0, 0, piece, 0)),
        ],
        out_specs=pl.BlockSpec((2, bins, width, channels), lambda i: (0, 0, 0, 0)),
        out_shape=jax.ShapeDtypeStruct((2, bins, width, channels), jnp.bfloat16),
        scratch_shapes=[pltpu.VMEM((bins + 2 * HALF, width, channels), jnp.float32)],
        compiler_params=pltpu.CompilerParams(vmem_limit_bytes=VMEM_LIMIT),
        cost_estimate=pl.CostEstimate(
            flops=20 * spectra.size // PIECES, bytes_accessed=4 * spectra.size // PIECES, transcendentals=spectra.size // PIECES
        ),
        name="whiten_piece",
    )(spectra, edges)


def cross_kernel(step, offsets, rank_ref, rows_ref, *refs):
    pieces, out_ref, wide_ref = refs[:PIECES], refs[PIECES], refs[PIECES + 1]
    sources, bins, width = rows_ref.shape
    windows = width // 2
    index = pl.program_id(0)

    @pl.when(index == 0)
    def _():
        for p, offset in enumerate(offsets):
            at = pl.multiple_of((rank_ref[0] ^ offset) * bins, bins)
            wide_ref[pl.ds(at, bins)] = rows_ref[p].astype(jnp.float32) * (1.0 / windows)

    sign = jnp.where(lax.broadcasted_iota(jnp.int32, (sources, width), 1) < windows, -1.0, 1.0)
    for k in range(step):
        f = index * step + k
        first = wide_ref[pl.ds(f, sources, stride=bins)]
        second = pltpu.roll(first, windows, 1) * sign
        left = jnp.concatenate([first, second], 0).astype(jnp.bfloat16)
        right = jnp.concatenate([piece[part, k] for part in range(2) for piece in pieces], 0)
        product = jnp.dot(left, right, preferred_element_type=jnp.float32).astype(jnp.bfloat16)
        out_ref[0, k] = product[:sources]
        out_ref[1, k] = product[sources:]


def cross_spectra(rows, offsets, rank, pieces):
    sources, bins, width = rows.shape
    channels = pieces[0].shape[-1]
    step = min(16, bins)
    return pl.pallas_call(
        functools.partial(cross_kernel, step, offsets),
        grid=(bins // step,),
        in_specs=[pl.BlockSpec(memory_space=pltpu.SMEM), pl.BlockSpec(rows.shape, lambda i: (0, 0, 0))]
        + [pl.BlockSpec((2, step, width // 2 // PIECES, channels), lambda i: (0, i, 0, 0))] * PIECES,
        out_specs=pl.BlockSpec((2, step, sources, channels), lambda i: (0, i, 0, 0)),
        out_shape=jax.ShapeDtypeStruct((2, bins, sources, channels), jnp.bfloat16),
        scratch_shapes=[pltpu.VMEM((sources * bins, width), jnp.float32)],
        compiler_params=pltpu.CompilerParams(vmem_limit_bytes=VMEM_LIMIT),
        name="cross_spectra",
    )(rank, rows, *pieces)


def gather_rows(row):
    count = lax.axis_size("rx")
    rank = lax.axis_index("rx")
    rows = row[None]
    bit = count // 2
    held = []
    while bit:
        other = lax.ppermute(rows, "rx", [(i, i ^ bit) for i in range(count)])
        rows = jnp.concatenate([rows, other], 0)
        held.append(bit)
        bit //= 2
    offsets = [sum(bit for k, bit in enumerate(held) if p >> k & 1) for p in range(count)]
    return rows, offsets


def local(spectra, source_index):
    channels_here = spectra.shape[3]
    rank = lax.axis_index("rx")
    column = lax.dynamic_slice(source_index, (rank,), (1,)) - rank * channels_here
    edges = edge_amplitudes(spectra)
    row = extract_row(spectra, column)
    rows, offsets = gather_rows(whiten_row(row, edges, column))
    pieces = [whiten_piece(spectra, edges, piece) for piece in range(PIECES)]
    return cross_spectra(rows, offsets, jnp.full((1,), rank, jnp.int32), pieces)


def solution(mesh):
    return jax.shard_map(
        local,
        mesh=mesh,
        in_specs=(P(None, "band", None, "rx"), P()),
        out_specs=P(None, "band", None, "rx"),
        check_vma=False,
    )
```

```python
import functools

import jax
import jax.numpy as jnp
from jax import lax
from jax.experimental import pallas as pl
from jax.experimental.pallas import tpu as pltpu
from jax.sharding import PartitionSpec as P

HALF = 4
SPAN = 2 * HALF + 1
FLOOR = 0.1
PIECES = 4
TINY = 1e-37
MIB = 1024 * 1024
VMEM = pl.BlockSpec(memory_space=pltpu.VMEM)
SMEM = pl.BlockSpec(memory_space=pltpu.SMEM)
HBM = pl.BlockSpec(memory_space=pltpu.HBM)


def params(mib=24):
    return pltpu.CompilerParams(vmem_limit_bytes=mib * MIB)


def amplitude_of(power):
    return (power * lax.rsqrt(jnp.maximum(power, TINY))).astype(jnp.bfloat16)


def dtype_of(shape, dtype=jnp.bfloat16):
    return jax.ShapeDtypeStruct(shape, dtype)


def edge_kernel(spectra_ref, *refs):
    outs, buffer, sem = refs[:-2], refs[-2], refs[-1]
    bins = spectra_ref.shape[1]
    for out in outs:
        if len(outs) == 2:
            start = bins - HALF if out is outs[0] else 0
        else:
            start = jnp.where(lax.axis_index("band") == 0, bins - HALF, 0)
        copy = pltpu.make_async_copy(spectra_ref.at[:, pl.ds(start, HALF)], buffer, sem)
        copy.start()
        copy.wait()
        real = buffer[0].astype(jnp.float32)
        imag = buffer[1].astype(jnp.float32)
        out[...] = amplitude_of(real * real + imag * imag)


def edge_amplitudes(spectra):
    count = lax.axis_size("band")
    _, _, windows, channels = spectra.shape
    ends = 1 if count == 2 else 2
    sent = pl.pallas_call(
        edge_kernel,
        in_specs=[HBM],
        out_specs=[VMEM] * ends,
        out_shape=[dtype_of((HALF, windows, channels))] * ends,
        scratch_shapes=[pltpu.VMEM((2, HALF, windows, channels), spectra.dtype), pltpu.SemaphoreType.DMA],
        compiler_params=params(48),
        name="edge_amplitude",
    )(spectra)
    if count == 2:
        received = lax.ppermute(sent[0], "band", [(0, 1), (1, 0)])
        return received, received
    below = lax.ppermute(sent[0], "band", [(i, i + 1) for i in range(count - 1)])
    above = lax.ppermute(sent[1], "band", [(i + 1, i) for i in range(count - 1)])
    return below, above


def inside(edge_refs, index):
    band, count = lax.axis_index("band"), lax.axis_size("band")
    below = edge_refs[0][index].astype(jnp.float32) * (band > 0).astype(jnp.float32)
    above = edge_refs[1][index].astype(jnp.float32) * (band < count - 1).astype(jnp.float32)
    return below, above


def select_column(column, blocks):
    lane = lax.broadcasted_iota(jnp.int32, (16, 256), 1)
    half = lax.broadcasted_iota(jnp.int32, (16, 256), 0) // 8
    picks = (lane == column + half * 128).astype(jnp.bfloat16)

    def scoped(*accumulators):
        for k, pair in enumerate(blocks):
            pltpu.matmul_push_rhs(jnp.concatenate(pair, 1), (k // 2) % 2, k % 2, transpose=True)
            pltpu.matmul_acc_lhs(accumulators[k], picks, load_staged_rhs=(k // 2) % 2)
        return [pltpu.matmul_pop(accumulator) for accumulator in accumulators]

    found = pl.run_scoped(scoped, *[pltpu.ACC(k % 2)((16, 256), jnp.float32) for k in range(len(blocks))])
    return [(both[:8], both[8:]) for both in found]


def rows_of(found, windows):
    left = lax.broadcasted_iota(jnp.int32, (8, 2 * windows), 1) < windows
    sublane = lax.broadcasted_iota(jnp.int32, (8, 2 * windows), 0)
    out = []
    for k in range(0, len(found), 2):
        total = jnp.zeros((8, 2 * windows), jnp.float32)
        for j in range(8):
            pair = found[k + j // 4]
            at = (j % 4) // 2 * 2 * windows
            real, imag = (part[:, at : at + 2 * windows] for part in pair)
            if j % 2 == 0:
                value = jnp.where(left, real, pltpu.roll(imag, windows, 1))
            else:
                value = jnp.where(left, pltpu.roll(real, windows, 1), imag)
            total = jnp.where(sublane == j, value, total)
        out.append(total)
    return out


def source_column(index_ref, channels):
    rank = lax.axis_index("rx")
    return index_ref[rank] - rank * channels


def extract_kernel(chunks, index_ref, spectra_ref, row_ref, total_ref, held_ref, amplitude_ref, sem):
    _, bins, windows, channels = spectra_ref.shape
    column = source_column(index_ref, channels)
    size = bins // chunks
    copies = []
    for k in range(chunks):
        part = (slice(None), pl.ds(k * size, size))
        copy = pltpu.make_async_copy(spectra_ref.at[part], held_ref.at[part], sem.at[k])
        copy.start()
        copies.append(copy)
    for k in range(chunks):
        copies[k].wait()
        blocks = []
        for f in range(k * size, (k + 1) * size, 4):
            blocks.append([held_ref[part, f : f + 4].reshape(4 * windows, channels) for part in range(2)])
        rows = rows_of(select_column(column, blocks), windows)
        row_ref[k * size : (k + 1) * size] = jnp.concatenate(rows, 0)
    values = row_ref[...]
    squares = values * values
    amplitude = amplitude_of(squares + pltpu.roll(squares, windows, 1)).astype(jnp.float32)
    amplitude_ref[0:8] = jnp.zeros((8, 2 * windows), jnp.float32)
    amplitude_ref[8 : bins + 8] = amplitude
    amplitude_ref[bins + 8 : bins + 16] = jnp.zeros((8, 2 * windows), jnp.float32)
    total = amplitude
    for k in range(1, HALF + 1):
        total = total + (amplitude_ref[8 - k : bins + 8 - k] + amplitude_ref[8 + k : bins + 8 + k])
    total_ref[...] = total


def extract_row(spectra, source_index):
    _, bins, windows, _ = spectra.shape
    chunks = min(8, bins // 8)
    return pl.pallas_call(
        functools.partial(extract_kernel, chunks),
        in_specs=[SMEM, HBM],
        out_specs=[VMEM] * 3,
        out_shape=[
            dtype_of((bins, 2 * windows), jnp.float32),
            dtype_of((bins, 2 * windows), jnp.float32),
            dtype_of(spectra.shape, spectra.dtype),
        ],
        scratch_shapes=[pltpu.VMEM((bins + 16, 2 * windows), jnp.float32), pltpu.SemaphoreType.DMA((chunks,))],
        compiler_params=params(48),
        cost_estimate=pl.CostEstimate(flops=0, bytes_accessed=4 * spectra.size, transcendentals=0),
        name="extract_row",
    )(source_index, spectra)


def whiten_row_kernel(index_ref, row_ref, total_ref, below_ref, above_ref, out_ref):
    bins, width = row_ref.shape
    _, windows, channels = below_ref.shape
    column = source_column(index_ref, channels)
    pair = [edge[...].reshape(HALF * windows, channels) for edge in (below_ref, above_ref)]
    ((below, above),) = select_column(column, [pair])
    band, count = lax.axis_index("band"), lax.axis_size("band")
    below = below * (band > 0).astype(jnp.float32)
    above = above * (band < count - 1).astype(jnp.float32)
    sublane = lax.broadcasted_iota(jnp.int32, (8, windows), 0)
    low = jnp.zeros((8, windows), jnp.float32)
    high = jnp.zeros((8, windows), jnp.float32)
    for j in range(HALF):
        part = slice(j * windows, (j + 1) * windows)
        low = low + jnp.where(sublane <= j, below[:, part], 0.0)
        high = high + jnp.where(sublane >= 8 - HALF + j, above[:, part], 0.0)
    low = jnp.concatenate([low, low], 1)
    high = jnp.concatenate([high, high], 1)
    total = jnp.concatenate([total_ref[:8] + low, total_ref[8 : bins - 8], total_ref[bins - 8 :] + high], 0)
    out_ref[0] = (row_ref[...] / (total * (1.0 / SPAN) + FLOOR)).astype(jnp.bfloat16)


def whiten_row(source_index, row, total, edges):
    return pl.pallas_call(
        whiten_row_kernel,
        in_specs=[SMEM] + [VMEM] * 4,
        out_specs=VMEM,
        out_shape=dtype_of((1,) + row.shape),
        compiler_params=params(),
        name="whiten_row",
    )(source_index, row, total, *edges)


def whiten_kernel(pieces, spectra_ref, below_ref, above_ref, *refs):
    outs, amplitude_ref = refs[-1 - len(pieces) : -1], refs[-1]
    bins = spectra_ref.shape[1]
    width = outs[0].shape[2]
    block = 16
    for piece, out_ref in zip(pieces, outs, strict=True):
        window = slice(piece * width, (piece + 1) * width)
        below, above = inside((below_ref, above_ref), (slice(None), window))
        amplitude_ref[0:HALF] = below
        amplitude_ref[bins + HALF : bins + 2 * HALF] = above

        @pl.loop(0, bins // block)
        def _(b):
            at = b * block
            real = spectra_ref[0, pl.ds(at, block), window].astype(jnp.float32)
            imag = spectra_ref[1, pl.ds(at, block), window].astype(jnp.float32)
            amplitude_ref[pl.ds(at + HALF, block)] = amplitude_of(real * real + imag * imag).astype(jnp.float32)

        @pl.loop(0, bins // block)
        def _(b):
            at = b * block
            one = [amplitude_ref[at + k] for k in range(block + 2 * HALF)]
            two = [one[k] + one[k + 1] for k in range(block + 2 * HALF - 1)]
            four = [two[k] + two[k + 2] for k in range(block + 2 * HALF - 3)]
            for k in range(block):
                total = (four[k] + four[k + 4]) + one[k + 8]
                scale = 1.0 / (total * (1.0 / SPAN) + FLOOR)
                for part in range(2):
                    value = spectra_ref[part, at + k, window].astype(jnp.float32)
                    out_ref[part, at + k] = (value * scale).astype(jnp.bfloat16)


def whiten_pieces(spectra, edges, pieces, after):
    _, bins, windows, channels = spectra.shape
    width = windows // PIECES
    share = len(pieces) * spectra.size // PIECES
    return pl.pallas_call(
        functools.partial(whiten_kernel, pieces),
        in_specs=[VMEM] * 4,
        out_specs=[VMEM] * len(pieces),
        out_shape=[dtype_of((2, bins, width, channels))] * len(pieces),
        scratch_shapes=[pltpu.VMEM((bins + 2 * HALF, width, channels), jnp.float32)],
        compiler_params=params(),
        cost_estimate=pl.CostEstimate(flops=20 * share, bytes_accessed=4 * share, transcendentals=share),
        name="whiten_windows",
    )(spectra, *edges, after)


def merge_kernel(mine_ref, other_ref, *refs):
    out_ref = refs[-1]
    rows = mine_ref.shape[0]
    out_ref[:rows] = mine_ref[...]
    out_ref[rows:] = other_ref[...]


def merge(mine, other, done):
    return pl.pallas_call(
        merge_kernel,
        in_specs=[VMEM] * (2 + len(done)),
        out_specs=VMEM,
        out_shape=dtype_of((2 * mine.shape[0],) + mine.shape[1:]),
        compiler_params=params(),
        name="merge_rows",
    )(mine, other, *done)


def cross_kernel(offsets, chunks, first_ref, second_ref, *refs):
    pieces, out_ref, wide_ref, buffer, sem = refs[:PIECES], *refs[PIECES:]
    half, bins, width = first_ref.shape
    windows = width // 2
    sources = 2 * half
    rank = lax.axis_index("rx")
    for p, offset in enumerate(offsets):
        at = pl.multiple_of((rank ^ offset) * bins, bins)
        row = first_ref[p] if p < half else second_ref[p - half]
        wide_ref[pl.ds(at, bins)] = row.astype(jnp.float32) * (1.0 / windows)
    sign = jnp.where(lax.broadcasted_iota(jnp.int32, (sources, width), 1) < windows, -1.0, 1.0)
    size = bins // chunks
    copies = []
    for chunk in range(chunks):
        for f in range(chunk * size, (chunk + 1) * size):
            first = wide_ref[pl.ds(f, sources, stride=bins)]
            second = pltpu.roll(first, windows, 1) * sign
            left = jnp.concatenate([first, second], 0).astype(jnp.bfloat16)
            right = jnp.concatenate([piece[part, f] for part in range(2) for piece in pieces], 0)
            product = jnp.dot(left, right, preferred_element_type=jnp.float32).astype(jnp.bfloat16)
            buffer[0, f] = product[:sources]
            buffer[1, f] = product[sources:]
        part = (slice(None), pl.ds(chunk * size, size))
        copy = pltpu.make_async_copy(buffer.at[part], out_ref.at[part], sem.at[chunk])
        copy.start()
        copies.append(copy)
    for copy in copies:
        copy.wait()


def cross_spectra(first, second, offsets, pieces):
    half, bins, width = first.shape
    sources = 2 * half
    channels = pieces[0].shape[-1]
    chunks = min(8, bins // 8)
    shape = (2, bins, sources, channels)
    return pl.pallas_call(
        functools.partial(cross_kernel, offsets, chunks),
        in_specs=[VMEM] * (2 + PIECES),
        out_specs=HBM,
        out_shape=dtype_of(shape),
        scratch_shapes=[
            pltpu.VMEM((sources * bins, width), jnp.float32),
            pltpu.VMEM(shape, jnp.bfloat16),
            pltpu.SemaphoreType.DMA((chunks,)),
        ],
        compiler_params=params(),
        name="cross_spectra",
    )(first, second, *pieces)


def local(spectra, source_index):
    edges = edge_amplitudes(spectra)
    row, total, held = extract_row(spectra, source_index)
    rows = whiten_row(source_index, row, total, edges)

    count = lax.axis_size("rx")
    bits = [1 << k for k in reversed(range(count.bit_length() - 1))]
    plan = {0: (0, 1), 1: (2, 3)}
    pieces = []
    other = None
    for step, bit in enumerate(bits):
        other = lax.ppermute(rows, "rx", [(i, i ^ bit) for i in range(count)])
        done = whiten_pieces(held, edges, plan[step], rows) if step in plan else []
        pieces += done
        if step < len(bits) - 1:
            rows = merge(rows, other, done)
    offsets = [sum(bit for k, bit in enumerate(bits) if p >> k & 1) for p in range(count)]
    return cross_spectra(rows, other, offsets, pieces)


def solution(mesh):
    def placed(spectra, source_index):
        with jax.sharding.use_abstract_mesh(mesh.abstract_mesh):
            return body(spectra, source_index)

    body = jax.shard_map(
        local,
        mesh=mesh,
        in_specs=(P(None, "band", None, "rx"), P()),
        out_specs=P(None, "band", None, "rx"),
        check_vma=False,
    )
    return placed
```

```python
import functools

import jax
import jax.numpy as jnp
from jax import lax
from jax.experimental import pallas as pl
from jax.experimental.pallas import tpu as pltpu
from jax.sharding import PartitionSpec as P

HALF = 4
SPAN = 2 * HALF + 1
FLOOR = 0.1
PIECES = 4
TINY = 1e-37
MIB = 1024 * 1024
VMEM = pl.BlockSpec(memory_space=pltpu.VMEM)
SMEM = pl.BlockSpec(memory_space=pltpu.SMEM)
HBM = pl.BlockSpec(memory_space=pltpu.HBM)


def params(mib=24):
    return pltpu.CompilerParams(vmem_limit_bytes=mib * MIB)


def amplitude_of(power):
    return (power * lax.rsqrt(jnp.maximum(power, TINY))).astype(jnp.bfloat16)


def dtype_of(shape, dtype=jnp.bfloat16):
    return jax.ShapeDtypeStruct(shape, dtype)


def edge_kernel(index_ref, spectra_ref, *refs):
    *out_refs, picks_ref, buffer, scalars, sem, index_sem = refs
    bins, channels = spectra_ref.shape[1], spectra_ref.shape[3]
    index_copy = pltpu.make_async_copy(index_ref, scalars, index_sem)
    index_copy.start()
    if len(out_refs) == 1:
        starts = [jnp.where(lax.axis_index("band") == 0, bins - HALF, 0)]
    else:
        starts = [bins - HALF, 0]
    copies = []
    for k, start in enumerate(starts):
        copy = pltpu.make_async_copy(spectra_ref.at[:, pl.ds(start, HALF)], buffer.at[k], sem.at[k])
        copy.start()
        copies.append(copy)
    index_copy.wait()
    rank = lax.axis_index("rx")
    column = scalars[rank] - rank * channels
    lane = lax.broadcasted_iota(jnp.int32, (16, 256), 1)
    half = lax.broadcasted_iota(jnp.int32, (16, 256), 0) // 8
    picks_ref[...] = (lane == column + half * channels).astype(jnp.bfloat16)
    for k, out_ref in enumerate(out_refs):
        copies[k].wait()
        real = buffer[k, 0].astype(jnp.float32)
        imag = buffer[k, 1].astype(jnp.float32)
        out_ref[...] = amplitude_of(real * real + imag * imag)


def edge_amplitudes(spectra, source_index):
    count = lax.axis_size("band")
    _, _, windows, channels = spectra.shape
    ends = 1 if count == 2 else 2
    *sent, picks = pl.pallas_call(
        edge_kernel,
        in_specs=[HBM, HBM],
        out_specs=[VMEM] * (ends + 1),
        out_shape=[dtype_of((HALF, windows, channels))] * ends + [dtype_of((16, 256))],
        scratch_shapes=[
            pltpu.VMEM((ends, 2, HALF, windows, channels), spectra.dtype),
            pltpu.SMEM(source_index.shape, source_index.dtype),
            pltpu.SemaphoreType.DMA((ends,)),
            pltpu.SemaphoreType.DMA,
        ],
        compiler_params=params(),
        name="edge_amplitude",
    )(source_index, spectra)
    if count == 2:
        received = lax.ppermute(sent[0], "band", [(0, 1), (1, 0)])
        return (received, received), picks
    below = lax.ppermute(sent[0], "band", [(i, i + 1) for i in range(count - 1)])
    above = lax.ppermute(sent[1], "band", [(i + 1, i) for i in range(count - 1)])
    return (below, above), picks


def inside(edge_refs, index):
    band, count = lax.axis_index("band"), lax.axis_size("band")
    below = edge_refs[0][index].astype(jnp.float32) * (band > 0).astype(jnp.float32)
    above = edge_refs[1][index].astype(jnp.float32) * (band < count - 1).astype(jnp.float32)
    return below, above


def select_column(picks, blocks):
    def scoped(*accumulators):
        for k, pair in enumerate(blocks):
            pltpu.matmul_push_rhs(jnp.concatenate(pair, 1), (k // 2) % 2, k % 2, transpose=True)
            pltpu.matmul_acc_lhs(accumulators[k], picks, load_staged_rhs=(k // 2) % 2)
        return [pltpu.matmul_pop(accumulator) for accumulator in accumulators]

    found = pl.run_scoped(scoped, *[pltpu.ACC(k % 2)((16, 256), jnp.float32) for k in range(len(blocks))])
    return [(both[:8], both[8:]) for both in found]


def rows_of(found, windows):
    left = lax.broadcasted_iota(jnp.int32, (8, 2 * windows), 1) < windows
    sublane = lax.broadcasted_iota(jnp.int32, (8, 2 * windows), 0)
    out = []
    for k in range(0, len(found), 2):
        total = jnp.zeros((8, 2 * windows), jnp.float32)
        for j in range(8):
            pair = found[k + j // 4]
            at = (j % 4) // 2 * 2 * windows
            real, imag = (part[:, at : at + 2 * windows] for part in pair)
            if j % 2 == 0:
                value = jnp.where(left, real, pltpu.roll(imag, windows, 1))
            else:
                value = jnp.where(left, pltpu.roll(real, windows, 1), imag)
            total = jnp.where(sublane == j, value, total)
        out.append(total)
    return out


def extract_kernel(chunks, picks_ref, spectra_ref, row_ref, total_ref, held_ref, amplitude_ref, sem):
    _, bins, windows, channels = spectra_ref.shape
    picks = picks_ref[...]
    size = bins // chunks
    copies = []
    for k in range(chunks):
        part = (slice(None), pl.ds(k * size, size))
        copy = pltpu.make_async_copy(spectra_ref.at[part], held_ref.at[part], sem.at[k])
        copy.start()
        copies.append(copy)
    for k in range(chunks):
        copies[k].wait()
        blocks = []
        for f in range(k * size, (k + 1) * size, 4):
            blocks.append([held_ref[part, f : f + 4].reshape(4 * windows, channels) for part in range(2)])
        rows = rows_of(select_column(picks, blocks), windows)
        row_ref[k * size : (k + 1) * size] = jnp.concatenate(rows, 0)
    values = row_ref[...]
    squares = values * values
    amplitude = amplitude_of(squares + pltpu.roll(squares, windows, 1)).astype(jnp.float32)
    amplitude_ref[0:8] = jnp.zeros((8, 2 * windows), jnp.float32)
    amplitude_ref[8 : bins + 8] = amplitude
    amplitude_ref[bins + 8 : bins + 16] = jnp.zeros((8, 2 * windows), jnp.float32)
    total = amplitude
    for k in range(1, HALF + 1):
        total = total + (amplitude_ref[8 - k : bins + 8 - k] + amplitude_ref[8 + k : bins + 8 + k])
    total_ref[...] = total


def extract_row(spectra, picks):
    _, bins, windows, _ = spectra.shape
    chunks = 2
    return pl.pallas_call(
        functools.partial(extract_kernel, chunks),
        in_specs=[VMEM, HBM],
        out_specs=[VMEM] * 3,
        out_shape=[
            dtype_of((bins, 2 * windows), jnp.float32),
            dtype_of((bins, 2 * windows), jnp.float32),
            dtype_of(spectra.shape, spectra.dtype),
        ],
        scratch_shapes=[pltpu.VMEM((bins + 16, 2 * windows), jnp.float32), pltpu.SemaphoreType.DMA((chunks,))],
        compiler_params=params(48),
        cost_estimate=pl.CostEstimate(flops=0, bytes_accessed=4 * spectra.size, transcendentals=0),
        name="extract_row",
    )(picks, spectra)


def whiten_row_kernel(picks_ref, row_ref, total_ref, below_ref, above_ref, out_ref):
    bins, width = row_ref.shape
    _, windows, channels = below_ref.shape
    pair = [edge[...].reshape(HALF * windows, channels) for edge in (below_ref, above_ref)]
    ((below, above),) = select_column(picks_ref[...], [pair])
    band, count = lax.axis_index("band"), lax.axis_size("band")
    below = below * (band > 0).astype(jnp.float32)
    above = above * (band < count - 1).astype(jnp.float32)
    sublane = lax.broadcasted_iota(jnp.int32, (8, windows), 0)
    low = jnp.zeros((8, windows), jnp.float32)
    high = jnp.zeros((8, windows), jnp.float32)
    for j in range(HALF):
        part = slice(j * windows, (j + 1) * windows)
        low = low + jnp.where(sublane <= j, below[:, part], 0.0)
        high = high + jnp.where(sublane >= 8 - HALF + j, above[:, part], 0.0)
    low = jnp.concatenate([low, low], 1)
    high = jnp.concatenate([high, high], 1)
    total = jnp.concatenate([total_ref[:8] + low, total_ref[8 : bins - 8], total_ref[bins - 8 :] + high], 0)
    out_ref[0] = (row_ref[...] / (total * (1.0 / SPAN) + FLOOR)).astype(jnp.bfloat16)


def whiten_row(picks, row, total, edges):
    return pl.pallas_call(
        whiten_row_kernel,
        in_specs=[VMEM] * 5,
        out_specs=VMEM,
        out_shape=dtype_of((1,) + row.shape),
        compiler_params=params(),
        name="whiten_row",
    )(picks, row, total, *edges)


def whiten_kernel(pieces, spectra_ref, below_ref, above_ref, *refs):
    outs, amplitude_ref = refs[-1 - len(pieces) : -1], refs[-1]
    bins = spectra_ref.shape[1]
    width = outs[0].shape[2]
    block = 16
    for piece, out_ref in zip(pieces, outs, strict=True):
        window = slice(piece * width, (piece + 1) * width)
        below, above = inside((below_ref, above_ref), (slice(None), window))
        amplitude_ref[0:HALF] = below
        amplitude_ref[bins + HALF : bins + 2 * HALF] = above

        @pl.loop(0, bins // block)
        def _(b):
            at = b * block
            real = spectra_ref[0, pl.ds(at, block), window].astype(jnp.float32)
            imag = spectra_ref[1, pl.ds(at, block), window].astype(jnp.float32)
            amplitude_ref[pl.ds(at + HALF, block)] = amplitude_of(real * real + imag * imag).astype(jnp.float32)

        @pl.loop(0, bins // block)
        def _(b):
            at = b * block
            one = [amplitude_ref[at + k] for k in range(block + 2 * HALF)]
            two = [one[k] + one[k + 1] for k in range(block + 2 * HALF - 1)]
            four = [two[k] + two[k + 2] for k in range(block + 2 * HALF - 3)]
            for k in range(block):
                total = (four[k] + four[k + 4]) + one[k + 8]
                scale = 1.0 / (total * (1.0 / SPAN) + FLOOR)
                for part in range(2):
                    value = spectra_ref[part, at + k, window].astype(jnp.float32)
                    out_ref[part, at + k] = (value * scale).astype(jnp.bfloat16)


def whiten_pieces(spectra, edges, pieces, after):
    _, bins, windows, channels = spectra.shape
    width = windows // PIECES
    share = len(pieces) * spectra.size // PIECES
    return pl.pallas_call(
        functools.partial(whiten_kernel, pieces),
        in_specs=[VMEM] * 4,
        out_specs=[VMEM] * len(pieces),
        out_shape=[dtype_of((2, bins, width, channels))] * len(pieces),
        scratch_shapes=[pltpu.VMEM((bins + 2 * HALF, width, channels), jnp.float32)],
        compiler_params=params(),
        cost_estimate=pl.CostEstimate(flops=20 * share, bytes_accessed=4 * share, transcendentals=share),
        name="whiten_windows",
    )(spectra, *edges, after)


def merge_kernel(mine_ref, other_ref, *refs):
    out_ref = refs[-1]
    rows = mine_ref.shape[0]
    out_ref[:rows] = mine_ref[...]
    out_ref[rows:] = other_ref[...]


def merge(mine, other, done):
    return pl.pallas_call(
        merge_kernel,
        in_specs=[VMEM] * (2 + len(done)),
        out_specs=VMEM,
        out_shape=dtype_of((2 * mine.shape[0],) + mine.shape[1:]),
        compiler_params=params(),
        name="merge_rows",
    )(mine, other, *done)


def cross_kernel(offsets, chunks, first_ref, second_ref, *refs):
    pieces, out_ref, wide_ref, buffer, sem = refs[:PIECES], *refs[PIECES:]
    half, bins, width = first_ref.shape
    windows = width // 2
    sources = 2 * half
    rank = lax.axis_index("rx")
    for p, offset in enumerate(offsets):
        at = pl.multiple_of((rank ^ offset) * bins, bins)
        row = first_ref[p] if p < half else second_ref[p - half]
        wide_ref[pl.ds(at, bins)] = row.astype(jnp.float32) * (1.0 / windows)
    sign = jnp.where(lax.broadcasted_iota(jnp.int32, (sources, width), 1) < windows, -1.0, 1.0)
    size = bins // chunks
    copies = []
    for chunk in range(chunks):
        for f in range(chunk * size, (chunk + 1) * size):
            first = wide_ref[pl.ds(f, sources, stride=bins)]
            second = pltpu.roll(first, windows, 1) * sign
            left = jnp.concatenate([first, second], 0).astype(jnp.bfloat16)
            right = jnp.concatenate([piece[part, f] for part in range(2) for piece in pieces], 0)
            product = jnp.dot(left, right, preferred_element_type=jnp.float32).astype(jnp.bfloat16)
            buffer[0, f] = product[:sources]
            buffer[1, f] = product[sources:]
        part = (slice(None), pl.ds(chunk * size, size))
        copy = pltpu.make_async_copy(buffer.at[part], out_ref.at[part], sem.at[chunk])
        copy.start()
        copies.append(copy)
    for copy in copies:
        copy.wait()


def cross_spectra(first, second, offsets, pieces):
    half, bins, width = first.shape
    sources = 2 * half
    channels = pieces[0].shape[-1]
    chunks = min(8, bins // 8)
    shape = (2, bins, sources, channels)
    return pl.pallas_call(
        functools.partial(cross_kernel, offsets, chunks),
        in_specs=[VMEM] * (2 + PIECES),
        out_specs=HBM,
        out_shape=dtype_of(shape),
        scratch_shapes=[
            pltpu.VMEM((sources * bins, width), jnp.float32),
            pltpu.VMEM(shape, jnp.bfloat16),
            pltpu.SemaphoreType.DMA((chunks,)),
        ],
        compiler_params=params(),
        name="cross_spectra",
    )(first, second, *pieces)


def local(spectra, source_index):
    spectra = pltpu.with_memory_space_constraint(spectra, pltpu.HBM)
    source_index = pltpu.with_memory_space_constraint(source_index, pltpu.HBM)
    edges, picks = edge_amplitudes(spectra, source_index)
    row, total, held = extract_row(spectra, picks)
    rows = whiten_row(picks, row, total, edges)

    count = lax.axis_size("rx")
    bits = [1 << k for k in reversed(range(count.bit_length() - 1))]
    plan = {0: (0, 1), 1: (2, 3)}
    pieces = []
    other = None
    for step, bit in enumerate(bits):
        other = lax.ppermute(rows, "rx", [(i, i ^ bit) for i in range(count)])
        done = whiten_pieces(held, edges, plan[step], rows) if step in plan else []
        pieces += done
        if step < len(bits) - 1:
            rows = merge(rows, other, done)
    offsets = [sum(bit for k, bit in enumerate(bits) if p >> k & 1) for p in range(count)]
    return cross_spectra(rows, other, offsets, pieces)


def solution(mesh):
    def placed(spectra, source_index):
        with jax.sharding.use_abstract_mesh(mesh.abstract_mesh):
            return body(spectra, source_index)

    body = jax.shard_map(
        local,
        mesh=mesh,
        in_specs=(P(None, "band", None, "rx"), P()),
        out_specs=P(None, "band", None, "rx"),
        check_vma=False,
    )
    return placed
```

```python
import functools

import jax
import jax.numpy as jnp
from jax import lax
from jax.experimental import pallas as pl
from jax.experimental.pallas import tpu as pltpu
from jax.sharding import PartitionSpec as P

HALF = 4
SPAN = 2 * HALF + 1
FLOOR = 0.1
PIECES = 4
TINY = 1e-37
MIB = 1024 * 1024
VMEM = pl.BlockSpec(memory_space=pltpu.VMEM)
SMEM = pl.BlockSpec(memory_space=pltpu.SMEM)
HBM = pl.BlockSpec(memory_space=pltpu.HBM)


def params(mib=24):
    return pltpu.CompilerParams(vmem_limit_bytes=mib * MIB)


def amplitude_of(power):
    return (power * lax.rsqrt(jnp.maximum(power, TINY))).astype(jnp.bfloat16)


def dtype_of(shape, dtype=jnp.bfloat16):
    return jax.ShapeDtypeStruct(shape, dtype)


def edge_kernel(index_ref, spectra_ref, *refs):
    *out_refs, picks_ref, buffer, scalars, sem, index_sem = refs
    bins, channels = spectra_ref.shape[1], spectra_ref.shape[3]
    index_copy = pltpu.make_async_copy(index_ref, scalars, index_sem)
    index_copy.start()
    if len(out_refs) == 1:
        starts = [jnp.where(lax.axis_index("band") == 0, bins - HALF, 0)]
    else:
        starts = [bins - HALF, 0]
    copies = []
    for k, start in enumerate(starts):
        copy = pltpu.make_async_copy(spectra_ref.at[:, pl.ds(start, HALF)], buffer.at[k], sem.at[k])
        copy.start()
        copies.append(copy)
    index_copy.wait()
    rank = lax.axis_index("rx")
    column = scalars[rank] - rank * channels
    lane = lax.broadcasted_iota(jnp.int32, (16, 256), 1)
    half = lax.broadcasted_iota(jnp.int32, (16, 256), 0) // 8
    picks_ref[...] = (lane == column + half * channels).astype(jnp.bfloat16)
    for k, out_ref in enumerate(out_refs):
        copies[k].wait()
        real = buffer[k, 0].astype(jnp.float32)
        imag = buffer[k, 1].astype(jnp.float32)
        out_ref[...] = amplitude_of(real * real + imag * imag)


def edge_amplitudes(spectra, source_index):
    count = lax.axis_size("band")
    _, _, windows, channels = spectra.shape
    ends = 1 if count == 2 else 2
    *sent, picks = pl.pallas_call(
        edge_kernel,
        in_specs=[HBM, HBM],
        out_specs=[VMEM] * (ends + 1),
        out_shape=[dtype_of((HALF, windows, channels))] * ends + [dtype_of((16, 256))],
        scratch_shapes=[
            pltpu.VMEM((ends, 2, HALF, windows, channels), spectra.dtype),
            pltpu.SMEM(source_index.shape, source_index.dtype),
            pltpu.SemaphoreType.DMA((ends,)),
            pltpu.SemaphoreType.DMA,
        ],
        compiler_params=params(),
        name="edge_amplitude",
    )(source_index, spectra)
    if count == 2:
        received = lax.ppermute(sent[0], "band", [(0, 1), (1, 0)])
        return (received, received), picks
    below = lax.ppermute(sent[0], "band", [(i, i + 1) for i in range(count - 1)])
    above = lax.ppermute(sent[1], "band", [(i + 1, i) for i in range(count - 1)])
    return (below, above), picks


def inside(edge_refs, index):
    band, count = lax.axis_index("band"), lax.axis_size("band")
    below = edge_refs[0][index].astype(jnp.float32) * (band > 0).astype(jnp.float32)
    above = edge_refs[1][index].astype(jnp.float32) * (band < count - 1).astype(jnp.float32)
    return below, above


def select_column(picks, blocks):
    def scoped(*accumulators):
        for k, pair in enumerate(blocks):
            pltpu.matmul_push_rhs(jnp.concatenate(pair, 1), (k // 2) % 2, k % 2, transpose=True)
            pltpu.matmul_acc_lhs(accumulators[k], picks, load_staged_rhs=(k // 2) % 2)
        return [pltpu.matmul_pop(accumulator) for accumulator in accumulators]

    found = pl.run_scoped(scoped, *[pltpu.ACC(k % 2)((16, 256), jnp.float32) for k in range(len(blocks))])
    return [(both[:8], both[8:]) for both in found]


def rows_of(found, windows):
    left = lax.broadcasted_iota(jnp.int32, (8, 2 * windows), 1) < windows
    sublane = lax.broadcasted_iota(jnp.int32, (8, 2 * windows), 0)
    out = []
    for k in range(0, len(found), 2):
        total = jnp.zeros((8, 2 * windows), jnp.float32)
        for j in range(8):
            pair = found[k + j // 4]
            at = (j % 4) // 2 * 2 * windows
            real, imag = (part[:, at : at + 2 * windows] for part in pair)
            if j % 2 == 0:
                value = jnp.where(left, real, pltpu.roll(imag, windows, 1))
            else:
                value = jnp.where(left, pltpu.roll(real, windows, 1), imag)
            total = jnp.where(sublane == j, value, total)
        out.append(total)
    return out


def extract_kernel(chunks, picks_ref, spectra_ref, row_ref, total_ref, held_ref, amplitude_ref, sem):
    _, bins, windows, channels = spectra_ref.shape
    picks = picks_ref[...]
    size = bins // chunks
    copies = []
    for k in range(chunks):
        part = (slice(None), pl.ds(k * size, size))
        copy = pltpu.make_async_copy(spectra_ref.at[part], held_ref.at[part], sem.at[k])
        copy.start()
        copies.append(copy)
    for k in range(chunks):
        copies[k].wait()
        blocks = []
        for f in range(k * size, (k + 1) * size, 4):
            blocks.append([held_ref[part, f : f + 4].reshape(4 * windows, channels) for part in range(2)])
        rows = rows_of(select_column(picks, blocks), windows)
        row_ref[k * size : (k + 1) * size] = jnp.concatenate(rows, 0)
    values = row_ref[...]
    squares = values * values
    amplitude = amplitude_of(squares + pltpu.roll(squares, windows, 1)).astype(jnp.float32)
    amplitude_ref[0:8] = jnp.zeros((8, 2 * windows), jnp.float32)
    amplitude_ref[8 : bins + 8] = amplitude
    amplitude_ref[bins + 8 : bins + 16] = jnp.zeros((8, 2 * windows), jnp.float32)
    total = amplitude
    for k in range(1, HALF + 1):
        total = total + (amplitude_ref[8 - k : bins + 8 - k] + amplitude_ref[8 + k : bins + 8 + k])
    total_ref[...] = total


def extract_row(spectra, picks):
    _, bins, windows, _ = spectra.shape
    chunks = 2
    return pl.pallas_call(
        functools.partial(extract_kernel, chunks),
        in_specs=[VMEM, HBM],
        out_specs=[VMEM] * 3,
        out_shape=[
            dtype_of((bins, 2 * windows), jnp.float32),
            dtype_of((bins, 2 * windows), jnp.float32),
            dtype_of(spectra.shape, spectra.dtype),
        ],
        scratch_shapes=[pltpu.VMEM((bins + 16, 2 * windows), jnp.float32), pltpu.SemaphoreType.DMA((chunks,))],
        compiler_params=params(48),
        cost_estimate=pl.CostEstimate(flops=0, bytes_accessed=4 * spectra.size, transcendentals=0),
        name="extract_row",
    )(picks, spectra)


def whiten_row_kernel(picks_ref, row_ref, total_ref, below_ref, above_ref, out_ref):
    bins, width = row_ref.shape
    _, windows, channels = below_ref.shape
    pair = [edge[...].reshape(HALF * windows, channels) for edge in (below_ref, above_ref)]
    ((below, above),) = select_column(picks_ref[...], [pair])
    band, count = lax.axis_index("band"), lax.axis_size("band")
    below = below * (band > 0).astype(jnp.float32)
    above = above * (band < count - 1).astype(jnp.float32)
    sublane = lax.broadcasted_iota(jnp.int32, (8, windows), 0)
    low = jnp.zeros((8, windows), jnp.float32)
    high = jnp.zeros((8, windows), jnp.float32)
    for j in range(HALF):
        part = slice(j * windows, (j + 1) * windows)
        low = low + jnp.where(sublane <= j, below[:, part], 0.0)
        high = high + jnp.where(sublane >= 8 - HALF + j, above[:, part], 0.0)
    low = jnp.concatenate([low, low], 1)
    high = jnp.concatenate([high, high], 1)
    total = jnp.concatenate([total_ref[:8] + low, total_ref[8 : bins - 8], total_ref[bins - 8 :] + high], 0)
    out_ref[0] = (row_ref[...] / (total * (1.0 / SPAN) + FLOOR)).astype(jnp.bfloat16)


def whiten_row(picks, row, total, edges):
    return pl.pallas_call(
        whiten_row_kernel,
        in_specs=[VMEM] * 5,
        out_specs=VMEM,
        out_shape=dtype_of((1,) + row.shape),
        compiler_params=params(),
        name="whiten_row",
    )(picks, row, total, *edges)


def whiten_kernel(pieces, spectra_ref, below_ref, above_ref, *refs):
    outs, amplitude_ref = refs[-1 - len(pieces) : -1], refs[-1]
    bins = spectra_ref.shape[1]
    width = outs[0].shape[2]
    block = 16
    for piece, out_ref in zip(pieces, outs, strict=True):
        window = slice(piece * width, (piece + 1) * width)
        below, above = inside((below_ref, above_ref), (slice(None), window))
        amplitude_ref[0:HALF] = below
        amplitude_ref[bins + HALF : bins + 2 * HALF] = above

        @pl.loop(0, bins // block)
        def _(b):
            at = b * block
            real = spectra_ref[0, pl.ds(at, block), window].astype(jnp.float32)
            imag = spectra_ref[1, pl.ds(at, block), window].astype(jnp.float32)
            amplitude_ref[pl.ds(at + HALF, block)] = amplitude_of(real * real + imag * imag).astype(jnp.float32)

        @pl.loop(0, bins // block)
        def _(b):
            at = b * block
            one = [amplitude_ref[at + k] for k in range(block + 2 * HALF)]
            two = [one[k] + one[k + 1] for k in range(block + 2 * HALF - 1)]
            four = [two[k] + two[k + 2] for k in range(block + 2 * HALF - 3)]
            for k in range(block):
                total = (four[k] + four[k + 4]) + one[k + 8]
                scale = 1.0 / (total * (1.0 / SPAN) + FLOOR)
                for part in range(2):
                    value = spectra_ref[part, at + k, window].astype(jnp.float32)
                    out_ref[part, at + k] = (value * scale).astype(jnp.bfloat16)


def whiten_pieces(spectra, edges, pieces, after):
    _, bins, windows, channels = spectra.shape
    width = windows // PIECES
    share = len(pieces) * spectra.size // PIECES
    return pl.pallas_call(
        functools.partial(whiten_kernel, pieces),
        in_specs=[VMEM] * 4,
        out_specs=[VMEM] * len(pieces),
        out_shape=[dtype_of((2, bins, width, channels))] * len(pieces),
        scratch_shapes=[pltpu.VMEM((bins + 2 * HALF, width, channels), jnp.float32)],
        compiler_params=params(),
        cost_estimate=pl.CostEstimate(flops=20 * share, bytes_accessed=4 * share, transcendentals=share),
        name="whiten_windows",
    )(spectra, *edges, after)


def merge_kernel(count, *refs):
    out_ref = refs[-1]
    at = 0
    for ref in refs[:count]:
        out_ref[at : at + ref.shape[0]] = ref[...]
        at += ref.shape[0]


def merge(blocks, done):
    return pl.pallas_call(
        functools.partial(merge_kernel, len(blocks)),
        in_specs=[VMEM] * (len(blocks) + len(done)),
        out_specs=VMEM,
        out_shape=dtype_of((sum(block.shape[0] for block in blocks),) + blocks[0].shape[1:]),
        compiler_params=params(),
        name="merge_rows",
    )(*blocks, *done)


def gather_rows(row, whiten):
    count = lax.axis_size("rx")
    bits = [1 << k for k in reversed(range(count.bit_length() - 1))]
    *far, near, across, core = bits

    def send(rows, bit):
        return lax.ppermute(rows, "rx", [(i, i ^ bit) for i in range(count)])

    def shifted(offsets, bit):
        return [offset ^ bit for offset in offsets]

    rows, held, pieces = row, [0], []
    for step, bit in enumerate(far):
        other = send(rows, bit)
        done = whiten((0, 1), rows) if step == 0 else []
        pieces += done
        rows = merge([rows, other], done)
        held = held + shifted(held, bit)
    others = [send(rows, bit) for bit in (near, across, near ^ across)]
    done = whiten((2, 3), rows)
    pieces += done
    rows = merge([rows, *others], done)
    held = held + shifted(held, near) + shifted(held, across) + shifted(shifted(held, near), across)
    blocks = [rows, send(rows, core)]
    offsets = held + shifted(held, core)
    return blocks, offsets, pieces


def cross_kernel(offsets, chunks, *refs):
    blocks, pieces, (out_ref, wide_ref, buffer, sem) = refs[: -4 - PIECES], refs[-4 - PIECES : -4], refs[-4:]
    sources = len(offsets)
    _, bins, width = blocks[0].shape
    windows = width // 2
    rank = lax.axis_index("rx")
    rows = [(ref, k) for ref in blocks for k in range(ref.shape[0])]
    for (ref, k), offset in zip(rows, offsets, strict=True):
        at = pl.multiple_of((rank ^ offset) * bins, bins)
        wide_ref[pl.ds(at, bins)] = ref[k].astype(jnp.float32) * (1.0 / windows)
    sign = jnp.where(lax.broadcasted_iota(jnp.int32, (sources, width), 1) < windows, -1.0, 1.0)
    size = bins // chunks
    copies = []
    for chunk in range(chunks):
        for f in range(chunk * size, (chunk + 1) * size):
            first = wide_ref[pl.ds(f, sources, stride=bins)]
            second = pltpu.roll(first, windows, 1) * sign
            left = jnp.concatenate([first, second], 0).astype(jnp.bfloat16)
            right = jnp.concatenate([piece[part, f] for part in range(2) for piece in pieces], 0)
            product = jnp.dot(left, right, preferred_element_type=jnp.float32).astype(jnp.bfloat16)
            buffer[0, f] = product[:sources]
            buffer[1, f] = product[sources:]
        part = (slice(None), pl.ds(chunk * size, size))
        copy = pltpu.make_async_copy(buffer.at[part], out_ref.at[part], sem.at[chunk])
        copy.start()
        copies.append(copy)
    for copy in copies:
        copy.wait()


def cross_spectra(blocks, offsets, pieces):
    sources = len(offsets)
    _, bins, width = blocks[0].shape
    channels = pieces[0].shape[-1]
    chunks = min(8, bins // 8)
    shape = (2, bins, sources, channels)
    return pl.pallas_call(
        functools.partial(cross_kernel, offsets, chunks),
        in_specs=[VMEM] * (len(blocks) + PIECES),
        out_specs=HBM,
        out_shape=dtype_of(shape),
        scratch_shapes=[
            pltpu.VMEM((sources * bins, width), jnp.float32),
            pltpu.VMEM(shape, jnp.bfloat16),
            pltpu.SemaphoreType.DMA((chunks,)),
        ],
        compiler_params=params(),
        name="cross_spectra",
    )(*blocks, *pieces)


def local(spectra, source_index):
    spectra = pltpu.with_memory_space_constraint(spectra, pltpu.HBM)
    source_index = pltpu.with_memory_space_constraint(source_index, pltpu.HBM)
    edges, picks = edge_amplitudes(spectra, source_index)
    row, total, held = extract_row(spectra, picks)
    rows = whiten_row(picks, row, total, edges)

    def whiten(piece, after):
        return whiten_pieces(held, edges, piece, after)

    return cross_spectra(*gather_rows(rows, whiten))


def solution(mesh):
    def placed(spectra, source_index):
        with jax.sharding.use_abstract_mesh(mesh.abstract_mesh):
            return body(spectra, source_index)

    body = jax.shard_map(
        local,
        mesh=mesh,
        in_specs=(P(None, "band", None, "rx"), P()),
        out_specs=P(None, "band", None, "rx"),
        check_vma=False,
    )
    return placed
```

```python
import functools

import jax
import jax.numpy as jnp
from jax import lax
from jax.experimental import pallas as pl
from jax.experimental.pallas import tpu as pltpu
from jax.sharding import PartitionSpec as P

HALF = 4
SPAN = 2 * HALF + 1
FLOOR = 0.1
TINY = 1e-37
MIB = 1024 * 1024
VMEM = pl.BlockSpec(memory_space=pltpu.VMEM)
SMEM = pl.BlockSpec(memory_space=pltpu.SMEM)
HBM = pl.BlockSpec(memory_space=pltpu.HBM)


def params(mib=24):
    return pltpu.CompilerParams(vmem_limit_bytes=mib * MIB)


def amplitude_of(power):
    return (power * lax.rsqrt(jnp.maximum(power, TINY))).astype(jnp.bfloat16)


def dtype_of(shape, dtype=jnp.bfloat16):
    return jax.ShapeDtypeStruct(shape, dtype)


def edge_kernel(index_ref, spectra_ref, *refs):
    *out_refs, picks_ref, buffer, scalars, sem, index_sem = refs
    ends = len(out_refs) // 2
    bins, channels = spectra_ref.shape[1], spectra_ref.shape[3]
    index_copy = pltpu.make_async_copy(index_ref, scalars, index_sem)
    index_copy.start()
    if ends == 1:
        starts = [jnp.where(lax.axis_index("band") == 0, bins - HALF, 0)]
    else:
        starts = [bins - HALF, 0]
    copies = []
    for k, start in enumerate(starts):
        copy = pltpu.make_async_copy(spectra_ref.at[:, pl.ds(start, HALF)], buffer.at[k], sem.at[k])
        copy.start()
        copies.append(copy)
    index_copy.wait()
    rank = lax.axis_index("rx")
    column = scalars[rank] - rank * channels
    row = lax.broadcasted_iota(jnp.int32, (256, 256), 0)
    lane = lax.broadcasted_iota(jnp.int32, (256, 256), 1)
    picks_ref[...] = (row == jnp.where(lane < channels, column, column + channels)).astype(jnp.bfloat16)
    pick = (lax.broadcasted_iota(jnp.int32, (16, 256), 1) == column).astype(jnp.bfloat16)
    for k in range(ends):
        copies[k].wait()
        real = buffer[k, 0].astype(jnp.float32)
        imag = buffer[k, 1].astype(jnp.float32)
        amplitude = amplitude_of(real * real + imag * imag)
        out_refs[k][...] = amplitude
        rows = amplitude.reshape(256, channels)
        pltpu.matmul_push_rhs(jnp.concatenate([rows, rows], 1), 0, 0, transpose=True)

        def scoped(accumulator):
            pltpu.matmul_acc_lhs(accumulator, pick, load_staged_rhs=0)
            return pltpu.matmul_pop(accumulator)

        column_of = pl.run_scoped(scoped, pltpu.ACC(0)((16, 256), jnp.float32))
        out_refs[ends + k][...] = column_of.astype(jnp.bfloat16)


def edge_amplitudes(spectra, source_index):
    count = lax.axis_size("band")
    _, _, windows, channels = spectra.shape
    ends = 1 if count == 2 else 2
    *sent, picks = pl.pallas_call(
        edge_kernel,
        in_specs=[HBM, HBM],
        out_specs=[VMEM] * (2 * ends + 1),
        out_shape=[dtype_of((HALF, windows, channels))] * ends + [dtype_of((16, HALF * windows))] * ends + [dtype_of((256, 256))],
        scratch_shapes=[
            pltpu.VMEM((ends, 2, HALF, windows, channels), spectra.dtype),
            pltpu.SMEM(source_index.shape, source_index.dtype),
            pltpu.SemaphoreType.DMA((ends,)),
            pltpu.SemaphoreType.DMA,
        ],
        compiler_params=params(),
        name="edge_amplitude",
    )(source_index, spectra)
    return sent[:ends], band_neighbours(sent[ends:]), picks


def band_neighbours(ends):
    count = lax.axis_size("band")
    if count == 2:
        received = lax.ppermute(ends[0], "band", [(0, 1), (1, 0)])
        return received, received
    below = lax.ppermute(ends[0], "band", [(i, i + 1) for i in range(count - 1)])
    above = lax.ppermute(ends[1], "band", [(i + 1, i) for i in range(count - 1)])
    return below, above


def select_column(spectra_ref, picks, start, count, spread_ref):
    windows, channels = spectra_ref.shape[2:]
    lane = lax.broadcasted_iota(jnp.int32, (windows, 2 * windows), 1)
    row = lax.broadcasted_iota(jnp.int32, (windows, 2 * windows), 0)
    masks = (lane == row, lane == row + windows)

    def scoped(*accumulators):
        for k, accumulator in enumerate(accumulators):
            both = jnp.concatenate([spectra_ref[0, start + k], spectra_ref[1, start + k]], 1)
            pltpu.matmul_acc_lhs(accumulator, both, load_staged_rhs=0 if picks[k % 2] else None)
            picks[k % 2] = False
        return [pltpu.matmul_pop(accumulator) for accumulator in accumulators]

    found = pl.run_scoped(scoped, *[pltpu.ACC(k % 2)((windows, 256), jnp.float32) for k in range(count)])
    for k, both in enumerate(found):
        total = jnp.zeros((8, 2 * windows), jnp.float32)
        for w in range(0, windows, 8):
            for part, mask in enumerate(masks):
                total = jnp.where(mask[w : w + 8], both[w : w + 8, part * channels : (part + 1) * channels], total)
        spread_ref[(start + k) * 8 : (start + k + 1) * 8] = total


def extract_kernel(chunks, picks_ref, spectra_ref, row_ref, total_ref, held_ref, spread_ref, amplitude_ref, sem):
    _, bins, windows, channels = spectra_ref.shape
    size = bins // chunks
    copies = []
    for k in range(chunks):
        part = (slice(None), pl.ds(k * size, size))
        copy = pltpu.make_async_copy(spectra_ref.at[part], held_ref.at[part], sem.at[k])
        copy.start()
        copies.append(copy)
    for unit in range(2):
        pltpu.matmul_push_rhs(picks_ref[...], 0, unit)
    staged = [True, True]
    for k in range(chunks):
        copies[k].wait()
        for start in range(k * size, (k + 1) * size, 16):
            select_column(held_ref, staged, start, 16, spread_ref)
            for f in range(start, start + 16, 8):
                rows = [spread_ref[pl.ds(f * 8 + j, 8, stride=8)] for j in range(8)]
                row_ref[f : f + 8] = sum(rows[1:], rows[0])
    values = row_ref[...]
    squares = values * values
    amplitude = amplitude_of(squares + pltpu.roll(squares, windows, 1)).astype(jnp.float32)
    amplitude_ref[0:8] = jnp.zeros((8, 2 * windows), jnp.float32)
    amplitude_ref[8 : bins + 8] = amplitude
    amplitude_ref[bins + 8 : bins + 16] = jnp.zeros((8, 2 * windows), jnp.float32)
    total = amplitude
    for k in range(1, HALF + 1):
        total = total + (amplitude_ref[8 - k : bins + 8 - k] + amplitude_ref[8 + k : bins + 8 + k])
    total_ref[...] = total


def extract_row(spectra, picks):
    _, bins, windows, _ = spectra.shape
    chunks = min(4, bins // 16)
    return pl.pallas_call(
        functools.partial(extract_kernel, chunks),
        in_specs=[VMEM, HBM],
        out_specs=[VMEM] * 3,
        out_shape=[
            dtype_of((bins, 2 * windows), jnp.float32),
            dtype_of((bins, 2 * windows), jnp.float32),
            dtype_of(spectra.shape, spectra.dtype),
        ],
        scratch_shapes=[pltpu.VMEM((8 * bins, 2 * windows), jnp.float32), pltpu.VMEM((bins + 16, 2 * windows), jnp.float32), pltpu.SemaphoreType.DMA((chunks,))],
        compiler_params=params(),
        cost_estimate=pl.CostEstimate(flops=0, bytes_accessed=4 * spectra.size, transcendentals=0),
        name="extract_row",
    )(picks, spectra)


def whiten_row_kernel(row_ref, total_ref, below_ref, above_ref, out_ref):
    bins, width = row_ref.shape
    windows = width // 2
    band, count = lax.axis_index("band"), lax.axis_size("band")
    below = below_ref[...].astype(jnp.float32)[:8] * (band > 0).astype(jnp.float32)
    above = above_ref[...].astype(jnp.float32)[:8] * (band < count - 1).astype(jnp.float32)
    sublane = lax.broadcasted_iota(jnp.int32, (8, windows), 0)
    low = jnp.zeros((8, windows), jnp.float32)
    high = jnp.zeros((8, windows), jnp.float32)
    for j in range(HALF):
        part = slice(j * windows, (j + 1) * windows)
        low = low + jnp.where(sublane <= j, below[:, part], 0.0)
        high = high + jnp.where(sublane >= 8 - HALF + j, above[:, part], 0.0)
    low = jnp.concatenate([low, low], 1)
    high = jnp.concatenate([high, high], 1)
    total = jnp.concatenate([total_ref[:8] + low, total_ref[8 : bins - 8], total_ref[bins - 8 :] + high], 0)
    out_ref[0] = (row_ref[...] / (total * (1.0 / SPAN) + FLOOR)).astype(jnp.bfloat16)


def whiten_row(row, total, columns):
    return pl.pallas_call(
        whiten_row_kernel,
        in_specs=[VMEM] * 4,
        out_specs=VMEM,
        out_shape=dtype_of((1,) + row.shape),
        compiler_params=params(),
        name="whiten_row",
    )(row, total, *columns)


def amplitude_kernel(first, spectra_ref, *refs):
    out_ref = refs[-1]
    bins = spectra_ref.shape[1]
    block = 16

    @pl.loop(0, bins // block)
    def _(b):
        at = pl.ds(b * block, block)
        for w in range(0, out_ref.shape[1], 16):
            window = slice(first + w, first + w + 16)
            real = spectra_ref[0, at, window].astype(jnp.float32)
            imag = spectra_ref[1, at, window].astype(jnp.float32)
            out_ref[at, w : w + 16] = amplitude_of(real * real + imag * imag).astype(jnp.float32)


def amplitudes(spectra, half, after):
    _, bins, windows, channels = spectra.shape
    share = spectra.size // 4
    return pl.pallas_call(
        functools.partial(amplitude_kernel, half * windows // 2),
        in_specs=[VMEM] * 2,
        out_specs=VMEM,
        out_shape=dtype_of((bins, windows // 2, channels), jnp.float32),
        compiler_params=params(),
        cost_estimate=pl.CostEstimate(flops=10 * share, bytes_accessed=4 * share, transcendentals=share),
        name="amplitude",
    )(spectra, after)


def whiten_kernel(spectra_ref, first_ref, second_ref, below_ref, above_ref, *refs):
    out_ref = refs[-1]
    _, bins, windows, _ = spectra_ref.shape
    band, count = lax.axis_index("band"), lax.axis_size("band")
    has_below = (band > 0).astype(jnp.float32)
    has_above = (band < count - 1).astype(jnp.float32)
    block = 16
    blocks = bins // block

    def one_block(b, w):
        at = b * block
        window = slice(w, w + 16)
        amplitude_ref, inner = (first_ref, w) if w < windows // 2 else (second_ref, w - windows // 2)
        one = []
        for k in range(-HALF, block + HALF):
            if isinstance(b, int) and at + k < 0:
                one.append(below_ref[HALF + k, window].astype(jnp.float32) * has_below)
            elif isinstance(b, int) and at + k >= bins:
                one.append(above_ref[at + k - bins, window].astype(jnp.float32) * has_above)
            else:
                one.append(amplitude_ref[at + k, inner : inner + 16])
        two = [one[k] + one[k + 1] for k in range(block + 2 * HALF - 1)]
        four = [two[k] + two[k + 2] for k in range(block + 2 * HALF - 3)]
        for k in range(block):
            total = (four[k] + four[k + 4]) + one[k + 8]
            scale = 1.0 / (total * (1.0 / SPAN) + FLOOR)
            for part in range(2):
                value = spectra_ref[part, at + k, window].astype(jnp.float32)
                out_ref[part, at + k, window] = (value * scale).astype(jnp.bfloat16)

    for w in range(0, windows, 16):
        one_block(0, w)
        one_block(blocks - 1, w)

        @pl.loop(1, blocks - 1)
        def _(b):
            one_block(b, w)


def whiten(spectra, halves, edges, after):
    return pl.pallas_call(
        whiten_kernel,
        in_specs=[VMEM] * (5 + len(after)),
        out_specs=VMEM,
        out_shape=dtype_of(spectra.shape),
        compiler_params=params(),
        cost_estimate=pl.CostEstimate(flops=7 * spectra.size, bytes_accessed=2 * spectra.size, transcendentals=spectra.size // 2),
        name="whiten_windows",
    )(spectra, *halves, *edges, *after)


def merge_kernel(count, *refs):
    out_ref = refs[-1]
    at = 0
    for ref in refs[:count]:
        out_ref[at : at + ref.shape[0]] = ref[...]
        at += ref.shape[0]


def merge(blocks, done):
    return pl.pallas_call(
        functools.partial(merge_kernel, len(blocks)),
        in_specs=[VMEM] * (len(blocks) + len(done)),
        out_specs=VMEM,
        out_shape=dtype_of((sum(block.shape[0] for block in blocks),) + blocks[0].shape[1:]),
        compiler_params=params(),
        name="merge_rows",
    )(*blocks, *done)


def send(rows, bit):
    count = lax.axis_size("rx")
    return lax.ppermute(rows, "rx", [(i, i ^ bit) for i in range(count)])


def shifted(offsets, bit):
    return [offset ^ bit for offset in offsets]


def gather_rows(row, spectra, ends):
    count = lax.axis_size("rx")
    *far, near, across, core = [1 << k for k in reversed(range(count.bit_length() - 1))]
    rows, held = row, [0]
    for bit in far[:-1]:
        rows = merge([rows, send(rows, bit)], [])
        held = held + shifted(held, bit)
    far = far[-1]
    from_far = send(rows, far)
    first = amplitudes(spectra, 0, rows)
    edges = band_neighbours([merge([end], [rows]) for end in ends])
    rows = merge([rows, from_far], [first])
    held = held + shifted(held, far)
    others = [send(rows, bit) for bit in (near ^ across, across, near)]
    second = amplitudes(spectra, 1, rows)
    whitened = whiten(spectra, (first, second), edges, [rows])
    rows = merge([rows, *others], [whitened])
    held = held + shifted(held, near ^ across) + shifted(held, across) + shifted(held, near)
    return [rows, send(rows, core)], held + shifted(held, core), whitened


def cross_kernel(offsets, chunks, *refs):
    *blocks, white_ref, out_ref, wide_ref, buffer, sem = refs
    sources = len(offsets)
    _, bins, width = blocks[0].shape
    windows = width // 2
    rank = lax.axis_index("rx")
    rows = [(ref, k) for ref in blocks for k in range(ref.shape[0])]
    for (ref, k), offset in zip(rows, offsets, strict=True):
        at = pl.multiple_of((rank ^ offset) * bins, bins)
        wide_ref[pl.ds(at, bins)] = ref[k].astype(jnp.float32) * (1.0 / windows)
    sign = jnp.where(lax.broadcasted_iota(jnp.int32, (sources, width), 1) < windows, -1.0, 1.0)
    size = bins // chunks
    copies = []
    for chunk in range(chunks):
        for f in range(chunk * size, (chunk + 1) * size):
            first = wide_ref[pl.ds(f, sources, stride=bins)]
            second = pltpu.roll(first, windows, 1) * sign
            left = jnp.concatenate([first, second], 0).astype(jnp.bfloat16)
            right = jnp.concatenate([white_ref[0, f], white_ref[1, f]], 0)
            product = jnp.dot(left, right, preferred_element_type=jnp.float32).astype(jnp.bfloat16)
            buffer[0, f] = product[:sources]
            buffer[1, f] = product[sources:]
        part = (slice(None), pl.ds(chunk * size, size))
        copy = pltpu.make_async_copy(buffer.at[part], out_ref.at[part], sem.at[chunk])
        copy.start()
        copies.append(copy)
    for copy in copies:
        copy.wait()


def cross_spectra(blocks, offsets, whitened):
    sources = len(offsets)
    _, bins, width = blocks[0].shape
    channels = whitened.shape[-1]
    chunks = min(8, bins // 8)
    shape = (2, bins, sources, channels)
    return pl.pallas_call(
        functools.partial(cross_kernel, offsets, chunks),
        in_specs=[VMEM] * (len(blocks) + 1),
        out_specs=HBM,
        out_shape=dtype_of(shape),
        scratch_shapes=[
            pltpu.VMEM((sources * bins, width), jnp.float32),
            pltpu.VMEM(shape, jnp.bfloat16),
            pltpu.SemaphoreType.DMA((chunks,)),
        ],
        compiler_params=params(),
        name="cross_spectra",
    )(*blocks, whitened)


def local(spectra, source_index):
    ends, columns, picks = edge_amplitudes(
        pltpu.with_memory_space_constraint(spectra, pltpu.HBM),
        pltpu.with_memory_space_constraint(source_index, pltpu.HBM),
    )
    row, total, held = extract_row(spectra, picks)
    return cross_spectra(*gather_rows(whiten_row(row, total, columns), held, ends))


def solution(mesh):
    def placed(spectra, source_index):
        with jax.sharding.use_abstract_mesh(mesh.abstract_mesh):
            return body(spectra, source_index)

    body = jax.shard_map(
        local,
        mesh=mesh,
        in_specs=(P(None, "band", None, "rx"), P()),
        out_specs=P(None, "band", None, "rx"),
        check_vma=False,
    )
    return placed
```

```python
import functools

import jax
import jax.numpy as jnp
from jax import lax
from jax.experimental import pallas as pl
from jax.experimental.pallas import tpu as pltpu
from jax.sharding import PartitionSpec as P

HALF = 4
SPAN = 2 * HALF + 1
FLOOR = 0.1
TINY = 1e-37
MIB = 1024 * 1024
VMEM = pl.BlockSpec(memory_space=pltpu.VMEM)
SMEM = pl.BlockSpec(memory_space=pltpu.SMEM)
HBM = pl.BlockSpec(memory_space=pltpu.HBM)


def params(mib=24):
    return pltpu.CompilerParams(vmem_limit_bytes=mib * MIB)


def amplitude_of(power):
    return (power * lax.rsqrt(jnp.maximum(power, TINY))).astype(jnp.bfloat16)


def dtype_of(shape, dtype=jnp.bfloat16):
    return jax.ShapeDtypeStruct(shape, dtype)


def window_masks(windows):
    lane = lax.broadcasted_iota(jnp.int32, (windows, 2 * windows), 1)
    row = lax.broadcasted_iota(jnp.int32, (windows, 2 * windows), 0)
    return lane == row, lane == row + windows


def edge_kernel(index_ref, spectra_ref, *refs):
    *out_refs, column_ref, scalars, sem, index_sem = refs
    ends = len(out_refs) // 2
    bins, windows, channels = spectra_ref.shape[1:]
    index_copy = pltpu.make_async_copy(index_ref, scalars, index_sem)
    index_copy.start()
    if ends == 1:
        starts = [jnp.where(lax.axis_index("band") == 0, bins - HALF, 0)]
    else:
        starts = [bins - HALF, 0]
    copies = []
    for k, start in enumerate(starts):
        for part in range(2):
            for j in range(HALF):
                copy = pltpu.make_async_copy(spectra_ref.at[part, start + j], out_refs[k].at[part, j], sem.at[len(copies)])
                copy.start()
                copies.append(copy)
    index_copy.wait()
    rank = lax.axis_index("rx")
    column = jnp.full(column_ref.shape, scalars[rank] - rank * channels, jnp.int32)
    column_ref[...] = column
    masks = window_masks(windows)
    for k in range(ends):
        for copy in copies[2 * HALF * k : 2 * HALF * (k + 1)]:
            copy.wait()
        real = out_refs[k][0].astype(jnp.float32)
        imag = out_refs[k][1].astype(jnp.float32)
        amplitude = amplitude_of(real * real + imag * imag).astype(jnp.float32)
        pairs = []
        for first in range(0, HALF, 2):
            total = jnp.zeros((8, 2 * windows), jnp.float32)
            for w in range(0, windows, 8):
                for part, mask in enumerate(masks):
                    value = jnp.take_along_axis(amplitude[first + part, w : w + 8], column, axis=1, mode="promise_in_bounds")
                    total = jnp.where(mask[w : w + 8], value, total)
            pairs.append(total)
        total = jnp.concatenate(pairs, 1)
        out_refs[ends + k][...] = jnp.concatenate([total, total], 0).astype(jnp.bfloat16)


def edge_amplitudes(spectra, source_index):
    count = lax.axis_size("band")
    _, _, windows, channels = spectra.shape
    ends = 1 if count == 2 else 2
    *sent, column = pl.pallas_call(
        edge_kernel,
        in_specs=[HBM, HBM],
        out_specs=[VMEM] * (2 * ends + 1),
        out_shape=[dtype_of((2, HALF, windows, channels))] * ends + [dtype_of((16, HALF * windows))] * ends
        + [dtype_of((8, channels), jnp.int32)],
        scratch_shapes=[
            pltpu.SMEM(source_index.shape, source_index.dtype),
            pltpu.SemaphoreType.DMA((2 * HALF * ends,)),
            pltpu.SemaphoreType.DMA,
        ],
        compiler_params=params(),
        name="edge_amplitude",
    )(source_index, spectra)
    return sent[:ends], band_neighbours(sent[ends:]), column


def end_kernel(end_ref, after_ref, out_ref):
    real = end_ref[0].astype(jnp.float32)
    imag = end_ref[1].astype(jnp.float32)
    out_ref[...] = amplitude_of(real * real + imag * imag)


def end_amplitudes(end, after):
    return pl.pallas_call(
        end_kernel,
        in_specs=[VMEM] * 2,
        out_specs=VMEM,
        out_shape=dtype_of(end.shape[1:]),
        compiler_params=params(),
        name="end_amplitude",
    )(end, after)


def band_neighbours(ends):
    count = lax.axis_size("band")
    if count == 2:
        received = lax.ppermute(ends[0], "band", [(0, 1), (1, 0)])
        return received, received
    below = lax.ppermute(ends[0], "band", [(i, i + 1) for i in range(count - 1)])
    above = lax.ppermute(ends[1], "band", [(i + 1, i) for i in range(count - 1)])
    return below, above


def select_column(spectra_ref, column, staged, start, count, spread_ref):
    windows, channels = spectra_ref.shape[2:]
    masks = window_masks(windows)
    halves = count // 2

    def scoped(*accumulators):
        for k, accumulator in enumerate(accumulators):
            both = jnp.concatenate([spectra_ref[0, start + k], spectra_ref[1, start + k]], 1)
            pltpu.matmul_acc_lhs(accumulator, both, load_staged_rhs=0 if staged[k % 2] else None)
            staged[k % 2] = False
        return [pltpu.matmul_pop(accumulator) for accumulator in accumulators]

    found = pl.run_scoped(scoped, *[pltpu.ACC(k % 2)((windows, 256), jnp.float32) for k in range(halves)])
    for k in range(count):
        total = jnp.zeros((8, 2 * windows), jnp.float32)
        if k >= halves:
            values = [spectra_ref[part, start + k].astype(jnp.float32) for part in range(2)]
        for w in range(0, windows, 8):
            for part, mask in enumerate(masks):
                if k < halves:
                    value = found[k][w : w + 8, part * channels : (part + 1) * channels]
                else:
                    value = jnp.take_along_axis(values[part][w : w + 8], column, axis=1, mode="promise_in_bounds")
                total = jnp.where(mask[w : w + 8], value, total)
        spread_ref[(start + k) * 8 : (start + k + 1) * 8] = total


def extract_kernel(chunks, column_ref, spectra_ref, row_ref, total_ref, spread_ref, amplitude_ref):
    _, bins, windows, channels = spectra_ref.shape
    size = bins // chunks
    column = column_ref[...]
    wide = jnp.concatenate([column] * (256 // 8), 0)
    row = lax.broadcasted_iota(jnp.int32, (256, channels), 0)
    picks = jnp.concatenate([(row == wide + part * channels).astype(jnp.bfloat16) for part in range(2)], 1)
    for unit in range(2):
        pltpu.matmul_push_rhs(picks, 0, unit)
    staged = [True, True]
    group = min(64, size)
    for k in range(chunks):
        for start in range(k * size, (k + 1) * size, group):
            select_column(spectra_ref, column, staged, start, group, spread_ref)
            for f in range(start, start + group, 8):
                rows = [spread_ref[pl.ds(f * 8 + j, 8, stride=8)] for j in range(8)]
                row_ref[f : f + 8] = sum(rows[1:], rows[0])
    values = row_ref[...]
    squares = values * values
    amplitude = amplitude_of(squares + pltpu.roll(squares, windows, 1)).astype(jnp.float32)
    amplitude_ref[0:8] = jnp.zeros((8, 2 * windows), jnp.float32)
    amplitude_ref[8 : bins + 8] = amplitude
    amplitude_ref[bins + 8 : bins + 16] = jnp.zeros((8, 2 * windows), jnp.float32)
    total = amplitude
    for k in range(1, HALF + 1):
        total = total + (amplitude_ref[8 - k : bins + 8 - k] + amplitude_ref[8 + k : bins + 8 + k])
    total_ref[...] = total


def extract_row(spectra, column):
    _, bins, windows, _ = spectra.shape
    chunks = max(bins // 64, 1)
    return pl.pallas_call(
        functools.partial(extract_kernel, chunks),
        in_specs=[VMEM] * 2,
        out_specs=[VMEM] * 2,
        out_shape=[
            dtype_of((bins, 2 * windows), jnp.float32),
            dtype_of((bins, 2 * windows), jnp.float32),
        ],
        scratch_shapes=[pltpu.VMEM((8 * bins, 2 * windows), jnp.float32), pltpu.VMEM((bins + 16, 2 * windows), jnp.float32)],
        compiler_params=params(),
        cost_estimate=pl.CostEstimate(flops=0, bytes_accessed=4 * spectra.size, transcendentals=0),
        name="extract_row",
    )(column, spectra)


def whiten_row_kernel(row_ref, total_ref, below_ref, above_ref, after_ref, out_ref):
    bins, width = row_ref.shape
    windows = width // 2
    band, count = lax.axis_index("band"), lax.axis_size("band")
    below = jnp.sum(below_ref[...].astype(jnp.float32)[:8], 0, keepdims=True) * (band > 0).astype(jnp.float32)
    above = jnp.sum(above_ref[...].astype(jnp.float32)[:8], 0, keepdims=True) * (band < count - 1).astype(jnp.float32)
    sublane = lax.broadcasted_iota(jnp.int32, (8, windows), 0)
    low = jnp.zeros((8, windows), jnp.float32)
    high = jnp.zeros((8, windows), jnp.float32)
    for j in range(HALF):
        part = slice(j * windows, (j + 1) * windows)
        low = low + jnp.where(sublane <= j, below[:, part], 0.0)
        high = high + jnp.where(sublane >= 8 - HALF + j, above[:, part], 0.0)
    low = jnp.concatenate([low, low], 1)
    high = jnp.concatenate([high, high], 1)
    total = jnp.concatenate([total_ref[:8] + low, total_ref[8 : bins - 8], total_ref[bins - 8 :] + high], 0)
    out_ref[0] = (row_ref[...] / (total * (1.0 / SPAN) + FLOOR)).astype(jnp.bfloat16)


def whiten_row(row, total, columns, after):
    return pl.pallas_call(
        whiten_row_kernel,
        in_specs=[VMEM] * 5,
        out_specs=VMEM,
        out_shape=dtype_of((1,) + row.shape),
        compiler_params=params(),
        name="whiten_row",
    )(row, total, *columns, after)


def amplitude_kernel(first, spectra_ref, *refs):
    out_ref = refs[-1]
    bins = spectra_ref.shape[1]
    block = 16

    @pl.loop(0, bins // block)
    def _(b):
        at = pl.ds(b * block, block)
        for w in range(0, out_ref.shape[1], 16):
            window = slice(first + w, first + w + 16)
            real = spectra_ref[0, at, window].astype(jnp.float32)
            imag = spectra_ref[1, at, window].astype(jnp.float32)
            out_ref[at, w : w + 16] = amplitude_of(real * real + imag * imag).astype(jnp.float32)


def amplitudes(spectra, half, after):
    _, bins, windows, channels = spectra.shape
    share = spectra.size // 4
    return pl.pallas_call(
        functools.partial(amplitude_kernel, half * windows // 2),
        in_specs=[VMEM] * 2,
        out_specs=VMEM,
        out_shape=dtype_of((bins, windows // 2, channels), jnp.float32),
        compiler_params=params(),
        cost_estimate=pl.CostEstimate(flops=10 * share, bytes_accessed=4 * share, transcendentals=share),
        name="amplitude",
    )(spectra, after)


def whiten_kernel(spectra_ref, first_ref, second_ref, below_ref, above_ref, *refs):
    out_ref = refs[-1]
    _, bins, windows, _ = spectra_ref.shape
    band, count = lax.axis_index("band"), lax.axis_size("band")
    has_below = (band > 0).astype(jnp.float32)
    has_above = (band < count - 1).astype(jnp.float32)
    block = 16
    blocks = bins // block

    def one_block(b, w):
        at = b * block
        window = slice(w, w + 16)
        amplitude_ref, inner = (first_ref, w) if w < windows // 2 else (second_ref, w - windows // 2)
        one = []
        for k in range(-HALF, block + HALF):
            if isinstance(b, int) and at + k < 0:
                one.append(below_ref[HALF + k, window].astype(jnp.float32) * has_below)
            elif isinstance(b, int) and at + k >= bins:
                one.append(above_ref[at + k - bins, window].astype(jnp.float32) * has_above)
            else:
                one.append(amplitude_ref[at + k, inner : inner + 16])
        two = [one[k] + one[k + 1] for k in range(block + 2 * HALF - 1)]
        four = [two[k] + two[k + 2] for k in range(block + 2 * HALF - 3)]
        for k in range(block):
            total = (four[k] + four[k + 4]) + one[k + 8]
            scale = 1.0 / (total * (1.0 / SPAN) + FLOOR)
            for part in range(2):
                value = spectra_ref[part, at + k, window].astype(jnp.float32)
                out_ref[part, at + k, window] = (value * scale).astype(jnp.bfloat16)

    for w in range(0, windows, 16):
        one_block(0, w)
        one_block(blocks - 1, w)

        @pl.loop(1, blocks - 1)
        def _(b):
            one_block(b, w)


def whiten(spectra, halves, edges, after):
    return pl.pallas_call(
        whiten_kernel,
        in_specs=[VMEM] * (5 + len(after)),
        out_specs=VMEM,
        out_shape=dtype_of(spectra.shape),
        compiler_params=params(),
        cost_estimate=pl.CostEstimate(flops=7 * spectra.size, bytes_accessed=2 * spectra.size, transcendentals=spectra.size // 2),
        name="whiten_windows",
    )(spectra, *halves, *edges, *after)


def merge_kernel(count, *refs):
    out_ref = refs[-1]
    at = 0
    for ref in refs[:count]:
        out_ref[at : at + ref.shape[0]] = ref[...]
        at += ref.shape[0]


def merge(blocks, done):
    return pl.pallas_call(
        functools.partial(merge_kernel, len(blocks)),
        in_specs=[VMEM] * (len(blocks) + len(done)),
        out_specs=VMEM,
        out_shape=dtype_of((sum(block.shape[0] for block in blocks),) + blocks[0].shape[1:]),
        compiler_params=params(),
        name="merge_rows",
    )(*blocks, *done)


def send(rows, bit):
    count = lax.axis_size("rx")
    return lax.ppermute(rows, "rx", [(i, i ^ bit) for i in range(count)])


def shifted(offsets, bit):
    return [offset ^ bit for offset in offsets]


def gather_rows(row, spectra, first, ends):
    count = lax.axis_size("rx")
    *far, near, across, core = [1 << k for k in reversed(range(count.bit_length() - 1))]
    rows, held = row, [0]
    for bit in far[:-1]:
        rows = merge([rows, send(rows, bit)], [])
        held = held + shifted(held, bit)
    far = far[-1]
    from_far = send(rows, far)
    edges = band_neighbours([end_amplitudes(end, rows) for end in ends])
    rows = merge([rows, from_far], [])
    held = held + shifted(held, far)
    others = [send(rows, bit) for bit in (near ^ across, across, near)]
    second = amplitudes(spectra, 1, rows)
    whitened = whiten(spectra, (first, second), edges, [rows])
    rows = merge([rows, *others], [whitened])
    held = held + shifted(held, near ^ across) + shifted(held, across) + shifted(held, near)
    return [rows, send(rows, core)], held + shifted(held, core), whitened


def cross_kernel(offsets, chunks, *refs):
    *blocks, white_ref, out_ref, wide_ref, buffer, sem = refs
    sources = len(offsets)
    _, bins, width = blocks[0].shape
    windows = width // 2
    rank = lax.axis_index("rx")
    rows = [(ref, k) for ref in blocks for k in range(ref.shape[0])]
    for (ref, k), offset in zip(rows, offsets, strict=True):
        at = pl.multiple_of((rank ^ offset) * bins, bins)
        wide_ref[pl.ds(at, bins)] = ref[k].astype(jnp.float32) * (1.0 / windows)
    sign = jnp.where(lax.broadcasted_iota(jnp.int32, (sources, width), 1) < windows, -1.0, 1.0)
    size = bins // chunks
    copies = []
    for chunk in range(chunks):
        for f in range(chunk * size, (chunk + 1) * size):
            first = wide_ref[pl.ds(f, sources, stride=bins)]
            second = pltpu.roll(first, windows, 1) * sign
            left = jnp.concatenate([first, second], 0).astype(jnp.bfloat16)
            right = jnp.concatenate([white_ref[0, f], white_ref[1, f]], 0)
            product = jnp.dot(left, right, preferred_element_type=jnp.float32).astype(jnp.bfloat16)
            buffer[0, f] = product[:sources]
            buffer[1, f] = product[sources:]
        part = (slice(None), pl.ds(chunk * size, size))
        copy = pltpu.make_async_copy(buffer.at[part], out_ref.at[part], sem.at[chunk])
        copy.start()
        copies.append(copy)
    for copy in copies:
        copy.wait()


def cross_spectra(blocks, offsets, whitened):
    sources = len(offsets)
    _, bins, width = blocks[0].shape
    channels = whitened.shape[-1]
    chunks = min(8, bins // 8)
    shape = (2, bins, sources, channels)
    return pl.pallas_call(
        functools.partial(cross_kernel, offsets, chunks),
        in_specs=[VMEM] * (len(blocks) + 1),
        out_specs=HBM,
        out_shape=dtype_of(shape),
        scratch_shapes=[
            pltpu.VMEM((sources * bins, width), jnp.float32),
            pltpu.VMEM(shape, jnp.bfloat16),
            pltpu.SemaphoreType.DMA((chunks,)),
        ],
        compiler_params=params(),
        name="cross_spectra",
    )(*blocks, whitened)


def local(spectra, source_index):
    ends, columns, column = edge_amplitudes(
        pltpu.with_memory_space_constraint(spectra, pltpu.HBM),
        pltpu.with_memory_space_constraint(source_index, pltpu.HBM),
    )
    row, total = extract_row(spectra, column)
    first = amplitudes(spectra, 0, row)
    return cross_spectra(*gather_rows(whiten_row(row, total, columns, first), spectra, first, ends))


def solution(mesh):
    def placed(spectra, source_index):
        with jax.sharding.use_abstract_mesh(mesh.abstract_mesh):
            return body(spectra, source_index)

    body = jax.shard_map(
        local,
        mesh=mesh,
        in_specs=(P(None, "band", None, "rx"), P()),
        out_specs=P(None, "band", None, "rx"),
        check_vma=False,
    )
    return placed
```

```python
import functools

import jax
import jax.numpy as jnp
from jax import lax
from jax.experimental import pallas as pl
from jax.experimental.pallas import tpu as pltpu
from jax.sharding import PartitionSpec as P

HALF = 4
SPAN = 2 * HALF + 1
FLOOR = 0.1
TINY = 1e-37
MIB = 1024 * 1024
VMEM = pl.BlockSpec(memory_space=pltpu.VMEM)
SMEM = pl.BlockSpec(memory_space=pltpu.SMEM)
HBM = pl.BlockSpec(memory_space=pltpu.HBM)


def params(mib=24):
    return pltpu.CompilerParams(vmem_limit_bytes=mib * MIB)


def amplitude_of(power):
    return (power * lax.rsqrt(jnp.maximum(power, TINY))).astype(jnp.bfloat16)


def dtype_of(shape, dtype=jnp.bfloat16):
    return jax.ShapeDtypeStruct(shape, dtype)


def window_masks(windows):
    lane = lax.broadcasted_iota(jnp.int32, (windows, 2 * windows), 1)
    row = lax.broadcasted_iota(jnp.int32, (windows, 2 * windows), 0)
    return lane == row, lane == row + windows


def edge_kernel(index_ref, spectra_ref, *refs):
    *out_refs, column_ref, scalars, sem, index_sem = refs
    ends = len(out_refs) // 2
    bins, windows, channels = spectra_ref.shape[1:]
    index_copy = pltpu.make_async_copy(index_ref, scalars, index_sem)
    index_copy.start()
    if ends == 1:
        starts = [jnp.where(lax.axis_index("band") == 0, bins - HALF, 0)]
    else:
        starts = [bins - HALF, 0]
    copies = []
    for k, start in enumerate(starts):
        for part in range(2):
            for j in range(HALF):
                copy = pltpu.make_async_copy(spectra_ref.at[part, start + j], out_refs[k].at[part, j], sem.at[len(copies)])
                copy.start()
                copies.append(copy)
    index_copy.wait()
    rank = lax.axis_index("rx")
    column = jnp.full(column_ref.shape, scalars[rank] - rank * channels, jnp.int32)
    column_ref[...] = column
    masks = window_masks(windows)
    for k in range(ends):
        for copy in copies[2 * HALF * k : 2 * HALF * (k + 1)]:
            copy.wait()
        real = out_refs[k][0].astype(jnp.float32)
        imag = out_refs[k][1].astype(jnp.float32)
        amplitude = amplitude_of(real * real + imag * imag).astype(jnp.float32)
        pairs = []
        for first in range(0, HALF, 2):
            total = jnp.zeros((8, 2 * windows), jnp.float32)
            for w in range(0, windows, 8):
                for part, mask in enumerate(masks):
                    value = jnp.take_along_axis(amplitude[first + part, w : w + 8], column, axis=1, mode="promise_in_bounds")
                    total = jnp.where(mask[w : w + 8], value, total)
            pairs.append(total)
        total = jnp.concatenate(pairs, 1)
        out_refs[ends + k][...] = jnp.concatenate([total, total], 0).astype(jnp.bfloat16)


def edge_amplitudes(spectra, source_index):
    count = lax.axis_size("band")
    _, _, windows, channels = spectra.shape
    ends = 1 if count == 2 else 2
    *sent, column = pl.pallas_call(
        edge_kernel,
        in_specs=[HBM, HBM],
        out_specs=[VMEM] * (2 * ends + 1),
        out_shape=[dtype_of((2, HALF, windows, channels))] * ends + [dtype_of((16, HALF * windows))] * ends
        + [dtype_of((8, channels), jnp.int32)],
        scratch_shapes=[
            pltpu.SMEM(source_index.shape, source_index.dtype),
            pltpu.SemaphoreType.DMA((2 * HALF * ends,)),
            pltpu.SemaphoreType.DMA,
        ],
        compiler_params=params(),
        name="edge_amplitude",
    )(source_index, spectra)
    return sent[:ends], band_neighbours(sent[ends:]), column


def end_kernel(end_ref, after_ref, out_ref):
    real = end_ref[0].astype(jnp.float32)
    imag = end_ref[1].astype(jnp.float32)
    out_ref[...] = amplitude_of(real * real + imag * imag)


def end_amplitudes(end, after):
    return pl.pallas_call(
        end_kernel,
        in_specs=[VMEM] * 2,
        out_specs=VMEM,
        out_shape=dtype_of(end.shape[1:]),
        compiler_params=params(),
        name="end_amplitude",
    )(end, after)


def band_neighbours(ends):
    count = lax.axis_size("band")
    if count == 2:
        received = lax.ppermute(ends[0], "band", [(0, 1), (1, 0)])
        return received, received
    below = lax.ppermute(ends[0], "band", [(i, i + 1) for i in range(count - 1)])
    above = lax.ppermute(ends[1], "band", [(i + 1, i) for i in range(count - 1)])
    return below, above


def select_column(spectra_ref, column, staged, start, count, spread_ref):
    windows, channels = spectra_ref.shape[2:]
    masks = window_masks(windows)
    halves = count // 2

    def scoped(*accumulators):
        for k, accumulator in enumerate(accumulators):
            both = jnp.concatenate([spectra_ref[0, start + k], spectra_ref[1, start + k]], 1)
            pltpu.matmul_acc_lhs(accumulator, both, load_staged_rhs=0 if staged[k % 2] else None)
            staged[k % 2] = False
        return [pltpu.matmul_pop(accumulator) for accumulator in accumulators]

    found = pl.run_scoped(scoped, *[pltpu.ACC(k % 2)((windows, 256), jnp.float32) for k in range(halves)])
    for k in range(count):
        total = jnp.zeros((8, 2 * windows), jnp.float32)
        if k >= halves:
            values = [spectra_ref[part, start + k].astype(jnp.float32) for part in range(2)]
        for w in range(0, windows, 8):
            for part, mask in enumerate(masks):
                if k < halves:
                    value = found[k][w : w + 8, part * channels : (part + 1) * channels]
                else:
                    value = jnp.take_along_axis(values[part][w : w + 8], column, axis=1, mode="promise_in_bounds")
                total = jnp.where(mask[w : w + 8], value, total)
        spread_ref[(start + k) * 8 : (start + k + 1) * 8] = total


def extract_kernel(chunks, column_ref, spectra_ref, row_ref, total_ref, spread_ref, amplitude_ref):
    _, bins, windows, channels = spectra_ref.shape
    size = bins // chunks
    column = column_ref[...]
    wide = jnp.concatenate([column] * (256 // 8), 0)
    row = lax.broadcasted_iota(jnp.int32, (256, channels), 0)
    picks = jnp.concatenate([(row == wide + part * channels).astype(jnp.bfloat16) for part in range(2)], 1)
    for unit in range(2):
        pltpu.matmul_push_rhs(picks, 0, unit)
    staged = [True, True]
    group = min(64, size)
    for k in range(chunks):
        for start in range(k * size, (k + 1) * size, group):
            select_column(spectra_ref, column, staged, start, group, spread_ref)
            for f in range(start, start + group, 8):
                rows = [spread_ref[pl.ds(f * 8 + j, 8, stride=8)] for j in range(8)]
                row_ref[f : f + 8] = sum(rows[1:], rows[0])
    values = row_ref[...]
    squares = values * values
    amplitude = amplitude_of(squares + pltpu.roll(squares, windows, 1)).astype(jnp.float32)
    amplitude_ref[0:8] = jnp.zeros((8, 2 * windows), jnp.float32)
    amplitude_ref[8 : bins + 8] = amplitude
    amplitude_ref[bins + 8 : bins + 16] = jnp.zeros((8, 2 * windows), jnp.float32)
    total = amplitude
    for k in range(1, HALF + 1):
        total = total + (amplitude_ref[8 - k : bins + 8 - k] + amplitude_ref[8 + k : bins + 8 + k])
    total_ref[...] = total


def extract_row(spectra, column):
    _, bins, windows, _ = spectra.shape
    chunks = max(bins // 64, 1)
    return pl.pallas_call(
        functools.partial(extract_kernel, chunks),
        in_specs=[VMEM] * 2,
        out_specs=[VMEM] * 2,
        out_shape=[
            dtype_of((bins, 2 * windows), jnp.float32),
            dtype_of((bins, 2 * windows), jnp.float32),
        ],
        scratch_shapes=[pltpu.VMEM((8 * bins, 2 * windows), jnp.float32), pltpu.VMEM((bins + 16, 2 * windows), jnp.float32)],
        compiler_params=params(),
        cost_estimate=pl.CostEstimate(flops=0, bytes_accessed=4 * spectra.size, transcendentals=0),
        name="extract_row",
    )(column, spectra)


def whiten_row_kernel(row_ref, total_ref, below_ref, above_ref, after_ref, out_ref):
    bins, width = row_ref.shape
    windows = width // 2
    band, count = lax.axis_index("band"), lax.axis_size("band")
    below = jnp.sum(below_ref[...].astype(jnp.float32)[:8], 0, keepdims=True) * (band > 0).astype(jnp.float32)
    above = jnp.sum(above_ref[...].astype(jnp.float32)[:8], 0, keepdims=True) * (band < count - 1).astype(jnp.float32)
    sublane = lax.broadcasted_iota(jnp.int32, (8, windows), 0)
    low = jnp.zeros((8, windows), jnp.float32)
    high = jnp.zeros((8, windows), jnp.float32)
    for j in range(HALF):
        part = slice(j * windows, (j + 1) * windows)
        low = low + jnp.where(sublane <= j, below[:, part], 0.0)
        high = high + jnp.where(sublane >= 8 - HALF + j, above[:, part], 0.0)
    low = jnp.concatenate([low, low], 1)
    high = jnp.concatenate([high, high], 1)
    total = jnp.concatenate([total_ref[:8] + low, total_ref[8 : bins - 8], total_ref[bins - 8 :] + high], 0)
    out_ref[0] = (row_ref[...] / (total * (1.0 / SPAN) + FLOOR)).astype(jnp.bfloat16)


def whiten_row(row, total, columns, after):
    return pl.pallas_call(
        whiten_row_kernel,
        in_specs=[VMEM] * 5,
        out_specs=VMEM,
        out_shape=dtype_of((1,) + row.shape),
        compiler_params=params(),
        name="whiten_row",
    )(row, total, *columns, after)


def amplitude_kernel(first, spectra_ref, *refs):
    out_ref = refs[-1]
    bins = spectra_ref.shape[1]
    block = 16

    @pl.loop(0, bins // block)
    def _(b):
        at = pl.ds(b * block, block)
        for w in range(0, out_ref.shape[1], 16):
            window = slice(first + w, first + w + 16)
            real = spectra_ref[0, at, window].astype(jnp.float32)
            imag = spectra_ref[1, at, window].astype(jnp.float32)
            out_ref[at, w : w + 16] = amplitude_of(real * real + imag * imag).astype(jnp.float32)


def amplitudes(spectra, half, after):
    _, bins, windows, channels = spectra.shape
    share = spectra.size // 4
    return pl.pallas_call(
        functools.partial(amplitude_kernel, half * windows // 2),
        in_specs=[VMEM] * 2,
        out_specs=VMEM,
        out_shape=dtype_of((bins, windows // 2, channels), jnp.float32),
        compiler_params=params(),
        cost_estimate=pl.CostEstimate(flops=10 * share, bytes_accessed=4 * share, transcendentals=share),
        name="amplitude",
    )(spectra, after)


def whiten_kernel(spectra_ref, first_ref, second_ref, below_ref, above_ref, *refs):
    out_ref = refs[-1]
    _, bins, windows, _ = spectra_ref.shape
    band, count = lax.axis_index("band"), lax.axis_size("band")
    has_below = (band > 0).astype(jnp.float32)
    has_above = (band < count - 1).astype(jnp.float32)
    block = 16
    blocks = bins // block

    def one_block(b, w):
        at = b * block
        window = slice(w, w + 16)
        amplitude_ref, inner = (first_ref, w) if w < windows // 2 else (second_ref, w - windows // 2)
        one = []
        for k in range(-HALF, block + HALF):
            if isinstance(b, int) and at + k < 0:
                one.append(below_ref[HALF + k, window].astype(jnp.float32) * has_below)
            elif isinstance(b, int) and at + k >= bins:
                one.append(above_ref[at + k - bins, window].astype(jnp.float32) * has_above)
            else:
                one.append(amplitude_ref[at + k, inner : inner + 16])
        two = [one[k] + one[k + 1] for k in range(block + 2 * HALF - 1)]
        four = [two[k] + two[k + 2] for k in range(block + 2 * HALF - 3)]
        for k in range(block):
            total = (four[k] + four[k + 4]) + one[k + 8]
            scale = 1.0 / (total * (1.0 / SPAN) + FLOOR)
            for part in range(2):
                value = spectra_ref[part, at + k, window].astype(jnp.float32)
                out_ref[part, at + k, window] = (value * scale).astype(jnp.bfloat16)

    for w in range(0, windows, 16):
        one_block(0, w)
        one_block(blocks - 1, w)

        @pl.loop(1, blocks - 1)
        def _(b):
            one_block(b, w)


def whiten(spectra, halves, edges, after):
    return pl.pallas_call(
        whiten_kernel,
        in_specs=[VMEM] * (5 + len(after)),
        out_specs=VMEM,
        out_shape=dtype_of(spectra.shape),
        compiler_params=params(),
        cost_estimate=pl.CostEstimate(flops=7 * spectra.size, bytes_accessed=2 * spectra.size, transcendentals=spectra.size // 2),
        name="whiten_windows",
    )(spectra, *halves, *edges, *after)


def merge_kernel(count, *refs):
    out_ref = refs[-1]
    at = 0
    for ref in refs[:count]:
        out_ref[at : at + ref.shape[0]] = ref[...]
        at += ref.shape[0]


def merge(blocks, done):
    return pl.pallas_call(
        functools.partial(merge_kernel, len(blocks)),
        in_specs=[VMEM] * (len(blocks) + len(done)),
        out_specs=VMEM,
        out_shape=dtype_of((sum(block.shape[0] for block in blocks),) + blocks[0].shape[1:]),
        compiler_params=params(),
        name="merge_rows",
    )(*blocks, *done)


def send(rows, bit):
    count = lax.axis_size("rx")
    return lax.ppermute(rows, "rx", [(i, i ^ bit) for i in range(count)])


def shifted(offsets, bit):
    return [offset ^ bit for offset in offsets]


def gather_rows(row, spectra, first, ends):
    count = lax.axis_size("rx")
    *far, near, across, core = [1 << k for k in reversed(range(count.bit_length() - 1))]
    rows, held = row, [0]
    for bit in far[:-1]:
        rows = merge([rows, send(rows, bit)], [])
        held = held + shifted(held, bit)
    far = far[-1]
    from_far = send(rows, far)
    edges = band_neighbours([end_amplitudes(end, rows) for end in ends])
    rows = merge([rows, from_far], [])
    held = held + shifted(held, far)
    others = [send(rows, bit) for bit in (near ^ across, across, near)]
    second = amplitudes(spectra, 1, rows)
    whitened = whiten(spectra, (first, second), edges, [rows])
    rows = merge([rows, *others], [whitened])
    held = held + shifted(held, near ^ across) + shifted(held, across) + shifted(held, near)
    return [rows, send(rows, core)], held + shifted(held, core), whitened


def cross_kernel(offsets, ends, *refs):
    *blocks, white_ref, out_ref, wide_ref, buffer, sem = refs
    sources = len(offsets)
    _, bins, width = blocks[0].shape
    windows = width // 2
    rank = lax.axis_index("rx")
    rows = [(ref, k) for ref in blocks for k in range(ref.shape[0])]
    pitch = wide_ref.shape[0] // sources
    for (ref, k), offset in zip(rows, offsets, strict=True):
        at = pl.multiple_of((rank ^ offset) * pitch, 8)
        wide_ref[pl.ds(at, bins)] = ref[k].astype(jnp.float32) * (1.0 / windows)
    sign = jnp.where(lax.broadcasted_iota(jnp.int32, (sources, width), 1) < windows, -1.0, 1.0)
    copies = []
    start = 0
    for end in ends:
        for f in range(start, end):
            first = wide_ref[pl.ds(f, sources, stride=pitch)]
            second = pltpu.roll(first, windows, 1) * sign
            left = jnp.concatenate([first, second], 0).astype(jnp.bfloat16)
            right = jnp.concatenate([white_ref[0, f], white_ref[1, f]], 0)
            product = jnp.dot(left, right, preferred_element_type=jnp.float32).astype(jnp.bfloat16)
            buffer[0, f] = product[:sources]
            buffer[1, f] = product[sources:]
        part = (slice(None), pl.ds(start, end - start))
        copy = pltpu.make_async_copy(buffer.at[part], out_ref.at[part], sem.at[len(copies)])
        copy.start()
        copies.append(copy)
        start = end
    for copy in copies:
        copy.wait()


def cross_spectra(blocks, offsets, whitened):
    sources = len(offsets)
    _, bins, width = blocks[0].shape
    channels = whitened.shape[-1]
    ends = [k * bins // 32 for k in (8, 16, 24, 30, 32)]
    shape = (2, bins, sources, channels)
    return pl.pallas_call(
        functools.partial(cross_kernel, offsets, ends),
        in_specs=[VMEM] * (len(blocks) + 1),
        out_specs=HBM,
        out_shape=dtype_of(shape),
        scratch_shapes=[
            pltpu.VMEM((sources * (bins + 8), width), jnp.float32),
            pltpu.VMEM(shape, jnp.bfloat16),
            pltpu.SemaphoreType.DMA((len(ends),)),
        ],
        compiler_params=params(),
        name="cross_spectra",
    )(*blocks, whitened)


def local(spectra, source_index):
    ends, columns, column = edge_amplitudes(
        pltpu.with_memory_space_constraint(spectra, pltpu.HBM),
        pltpu.with_memory_space_constraint(source_index, pltpu.HBM),
    )
    row, total = extract_row(spectra, column)
    first = amplitudes(spectra, 0, row)
    return cross_spectra(*gather_rows(whiten_row(row, total, columns, first), spectra, first, ends))


def solution(mesh):
    def placed(spectra, source_index):
        with jax.sharding.use_abstract_mesh(mesh.abstract_mesh):
            return body(spectra, source_index)

    body = jax.shard_map(
        local,
        mesh=mesh,
        in_specs=(P(None, "band", None, "rx"), P()),
        out_specs=P(None, "band", None, "rx"),
        check_vma=False,
    )
    return placed
```

```python
import functools

import jax
import jax.numpy as jnp
from jax import lax
from jax.experimental import pallas as pl
from jax.experimental.pallas import tpu as pltpu
from jax.sharding import PartitionSpec as P

HALF = 4
SPAN = 2 * HALF + 1
FLOOR = 0.1
TINY = 1e-37
MIB = 1024 * 1024
VMEM = pl.BlockSpec(memory_space=pltpu.VMEM)
SMEM = pl.BlockSpec(memory_space=pltpu.SMEM)
HBM = pl.BlockSpec(memory_space=pltpu.HBM)


def params(mib=24):
    return pltpu.CompilerParams(vmem_limit_bytes=mib * MIB)


def amplitude_of(power):
    return (power * lax.rsqrt(jnp.maximum(power, TINY))).astype(jnp.bfloat16)


def dtype_of(shape, dtype=jnp.bfloat16):
    return jax.ShapeDtypeStruct(shape, dtype)


def window_masks(windows):
    lane = lax.broadcasted_iota(jnp.int32, (windows, 2 * windows), 1)
    row = lax.broadcasted_iota(jnp.int32, (windows, 2 * windows), 0)
    return lane == row, lane == row + windows


def edge_kernel(index_ref, spectra_ref, *refs):
    *out_refs, column_ref, scalars, sem, index_sem = refs
    ends = len(out_refs) // 2
    bins, windows, channels = spectra_ref.shape[1:]
    index_copy = pltpu.make_async_copy(index_ref, scalars, index_sem)
    index_copy.start()
    if ends == 1:
        starts = [jnp.where(lax.axis_index("band") == 0, bins - HALF, 0)]
    else:
        starts = [bins - HALF, 0]
    copies = []
    for k, start in enumerate(starts):
        for part in range(2):
            for j in range(HALF):
                copy = pltpu.make_async_copy(spectra_ref.at[part, start + j], out_refs[k].at[part, j], sem.at[len(copies)])
                copy.start()
                copies.append(copy)
    index_copy.wait()
    rank = lax.axis_index("rx")
    column = jnp.full(column_ref.shape, scalars[rank] - rank * channels, jnp.int32)
    column_ref[...] = column
    masks = window_masks(windows)
    for k in range(ends):
        for copy in copies[2 * HALF * k : 2 * HALF * (k + 1)]:
            copy.wait()
        real = out_refs[k][0].astype(jnp.float32)
        imag = out_refs[k][1].astype(jnp.float32)
        amplitude = amplitude_of(real * real + imag * imag).astype(jnp.float32)
        pairs = []
        for first in range(0, HALF, 2):
            total = jnp.zeros((8, 2 * windows), jnp.float32)
            for w in range(0, windows, 8):
                for part, mask in enumerate(masks):
                    value = jnp.take_along_axis(amplitude[first + part, w : w + 8], column, axis=1, mode="promise_in_bounds")
                    total = jnp.where(mask[w : w + 8], value, total)
            pairs.append(total)
        total = jnp.concatenate(pairs, 1)
        out_refs[ends + k][...] = jnp.concatenate([total, total], 0).astype(jnp.bfloat16)


def edge_amplitudes(spectra, source_index):
    count = lax.axis_size("band")
    _, _, windows, channels = spectra.shape
    ends = 1 if count == 2 else 2
    *sent, column = pl.pallas_call(
        edge_kernel,
        in_specs=[HBM, HBM],
        out_specs=[VMEM] * (2 * ends + 1),
        out_shape=[dtype_of((2, HALF, windows, channels))] * ends + [dtype_of((16, HALF * windows))] * ends
        + [dtype_of((8, channels), jnp.int32)],
        scratch_shapes=[
            pltpu.SMEM(source_index.shape, source_index.dtype),
            pltpu.SemaphoreType.DMA((2 * HALF * ends,)),
            pltpu.SemaphoreType.DMA,
        ],
        compiler_params=params(),
        name="edge_amplitude",
    )(source_index, spectra)
    return sent[:ends], band_neighbours(sent[ends:]), column


def end_kernel(end_ref, after_ref, out_ref):
    real = end_ref[0].astype(jnp.float32)
    imag = end_ref[1].astype(jnp.float32)
    out_ref[...] = amplitude_of(real * real + imag * imag)


def end_amplitudes(end, after):
    return pl.pallas_call(
        end_kernel,
        in_specs=[VMEM] * 2,
        out_specs=VMEM,
        out_shape=dtype_of(end.shape[1:]),
        compiler_params=params(),
        name="end_amplitude",
    )(end, after)


def band_neighbours(ends):
    count = lax.axis_size("band")
    if count == 2:
        received = lax.ppermute(ends[0], "band", [(0, 1), (1, 0)])
        return received, received
    below = lax.ppermute(ends[0], "band", [(i, i + 1) for i in range(count - 1)])
    above = lax.ppermute(ends[1], "band", [(i + 1, i) for i in range(count - 1)])
    return below, above


def select_column(spectra_ref, column, staged, start, count, spread_ref):
    windows, channels = spectra_ref.shape[2:]
    masks = window_masks(windows)
    halves = count // 2

    def scoped(*accumulators):
        for k, accumulator in enumerate(accumulators):
            both = jnp.concatenate([spectra_ref[0, start + k], spectra_ref[1, start + k]], 1)
            pltpu.matmul_acc_lhs(accumulator, both, load_staged_rhs=0 if staged[k % 2] else None)
            staged[k % 2] = False
        return [pltpu.matmul_pop(accumulator) for accumulator in accumulators]

    found = pl.run_scoped(scoped, *[pltpu.ACC(k % 2)((windows, 256), jnp.float32) for k in range(halves)])
    for k in range(count):
        total = jnp.zeros((8, 2 * windows), jnp.float32)
        if k >= halves:
            values = [spectra_ref[part, start + k].astype(jnp.float32) for part in range(2)]
        for w in range(0, windows, 8):
            for part, mask in enumerate(masks):
                if k < halves:
                    value = found[k][w : w + 8, part * channels : (part + 1) * channels]
                else:
                    value = jnp.take_along_axis(values[part][w : w + 8], column, axis=1, mode="promise_in_bounds")
                total = jnp.where(mask[w : w + 8], value, total)
        spread_ref[(start + k) * 8 : (start + k + 1) * 8] = total


def extract_kernel(chunks, column_ref, spectra_ref, row_ref, total_ref, spread_ref, amplitude_ref):
    _, bins, windows, channels = spectra_ref.shape
    size = bins // chunks
    column = column_ref[...]
    wide = jnp.concatenate([column] * (256 // 8), 0)
    row = lax.broadcasted_iota(jnp.int32, (256, channels), 0)
    picks = jnp.concatenate([(row == wide + part * channels).astype(jnp.bfloat16) for part in range(2)], 1)
    for unit in range(2):
        pltpu.matmul_push_rhs(picks, 0, unit)
    staged = [True, True]
    group = min(64, size)
    for k in range(chunks):
        for start in range(k * size, (k + 1) * size, group):
            select_column(spectra_ref, column, staged, start, group, spread_ref)
            for f in range(start, start + group, 8):
                rows = [spread_ref[pl.ds(f * 8 + j, 8, stride=8)] for j in range(8)]
                row_ref[f : f + 8] = sum(rows[1:], rows[0])
    values = row_ref[...]
    squares = values * values
    amplitude = amplitude_of(squares + pltpu.roll(squares, windows, 1)).astype(jnp.float32)
    amplitude_ref[0:8] = jnp.zeros((8, 2 * windows), jnp.float32)
    amplitude_ref[8 : bins + 8] = amplitude
    amplitude_ref[bins + 8 : bins + 16] = jnp.zeros((8, 2 * windows), jnp.float32)
    total = amplitude
    for k in range(1, HALF + 1):
        total = total + (amplitude_ref[8 - k : bins + 8 - k] + amplitude_ref[8 + k : bins + 8 + k])
    total_ref[...] = total


def extract_row(spectra, column):
    _, bins, windows, _ = spectra.shape
    chunks = max(bins // 64, 1)
    return pl.pallas_call(
        functools.partial(extract_kernel, chunks),
        in_specs=[VMEM] * 2,
        out_specs=[VMEM] * 2,
        out_shape=[
            dtype_of((bins, 2 * windows), jnp.float32),
            dtype_of((bins, 2 * windows), jnp.float32),
        ],
        scratch_shapes=[pltpu.VMEM((8 * bins, 2 * windows), jnp.float32), pltpu.VMEM((bins + 16, 2 * windows), jnp.float32)],
        compiler_params=params(),
        cost_estimate=pl.CostEstimate(flops=0, bytes_accessed=4 * spectra.size, transcendentals=0),
        name="extract_row",
    )(column, spectra)


def whiten_row_kernel(row_ref, total_ref, below_ref, above_ref, after_ref, out_ref):
    bins, width = row_ref.shape
    windows = width // 2
    band, count = lax.axis_index("band"), lax.axis_size("band")
    below = jnp.sum(below_ref[...].astype(jnp.float32)[:8], 0, keepdims=True) * (band > 0).astype(jnp.float32)
    above = jnp.sum(above_ref[...].astype(jnp.float32)[:8], 0, keepdims=True) * (band < count - 1).astype(jnp.float32)
    sublane = lax.broadcasted_iota(jnp.int32, (8, windows), 0)
    low = jnp.zeros((8, windows), jnp.float32)
    high = jnp.zeros((8, windows), jnp.float32)
    for j in range(HALF):
        part = slice(j * windows, (j + 1) * windows)
        low = low + jnp.where(sublane <= j, below[:, part], 0.0)
        high = high + jnp.where(sublane >= 8 - HALF + j, above[:, part], 0.0)
    low = jnp.concatenate([low, low], 1)
    high = jnp.concatenate([high, high], 1)
    total = jnp.concatenate([total_ref[:8] + low, total_ref[8 : bins - 8], total_ref[bins - 8 :] + high], 0)
    out_ref[0] = (row_ref[...] / (total * (1.0 / SPAN) + FLOOR)).astype(jnp.bfloat16)


def whiten_row(row, total, columns, after):
    return pl.pallas_call(
        whiten_row_kernel,
        in_specs=[VMEM] * 5,
        out_specs=VMEM,
        out_shape=dtype_of((1,) + row.shape),
        compiler_params=params(),
        name="whiten_row",
    )(row, total, *columns, after)


def amplitude_kernel(first, spectra_ref, *refs):
    out_ref = refs[-1]
    bins = spectra_ref.shape[1]
    block = 16

    @pl.loop(0, bins // block)
    def _(b):
        at = pl.ds(b * block, block)
        for w in range(0, out_ref.shape[1], 16):
            window = slice(first + w, first + w + 16)
            real = spectra_ref[0, at, window].astype(jnp.float32)
            imag = spectra_ref[1, at, window].astype(jnp.float32)
            out_ref[at, w : w + 16] = amplitude_of(real * real + imag * imag).astype(jnp.float32)


def amplitudes(spectra, half, after):
    _, bins, windows, channels = spectra.shape
    share = spectra.size // 4
    return pl.pallas_call(
        functools.partial(amplitude_kernel, half * windows // 2),
        in_specs=[VMEM] * 2,
        out_specs=VMEM,
        out_shape=dtype_of((bins, windows // 2, channels), jnp.float32),
        compiler_params=params(),
        cost_estimate=pl.CostEstimate(flops=10 * share, bytes_accessed=4 * share, transcendentals=share),
        name="amplitude",
    )(spectra, after)


def whiten_kernel(spectra_ref, first_ref, second_ref, below_ref, above_ref, *refs):
    out_ref = refs[-1]
    _, bins, windows, _ = spectra_ref.shape
    band, count = lax.axis_index("band"), lax.axis_size("band")
    has_below = (band > 0).astype(jnp.float32)
    has_above = (band < count - 1).astype(jnp.float32)
    block = 16
    blocks = bins // block

    def one_block(b, w):
        at = b * block
        window = slice(w, w + 16)
        amplitude_ref, inner = (first_ref, w) if w < windows // 2 else (second_ref, w - windows // 2)
        one = []
        for k in range(-HALF, block + HALF):
            if isinstance(b, int) and at + k < 0:
                one.append(below_ref[HALF + k, window].astype(jnp.float32) * has_below)
            elif isinstance(b, int) and at + k >= bins:
                one.append(above_ref[at + k - bins, window].astype(jnp.float32) * has_above)
            else:
                one.append(amplitude_ref[at + k, inner : inner + 16])
        two = [one[k] + one[k + 1] for k in range(block + 2 * HALF - 1)]
        four = [two[k] + two[k + 2] for k in range(block + 2 * HALF - 3)]
        for k in range(block):
            total = (four[k] + four[k + 4]) + one[k + 8]
            scale = 1.0 / (total * (1.0 / SPAN) + FLOOR)
            for part in range(2):
                value = spectra_ref[part, at + k, window].astype(jnp.float32)
                out_ref[part, at + k, window] = (value * scale).astype(jnp.bfloat16)

    for w in range(0, windows, 16):
        one_block(0, w)
        one_block(blocks - 1, w)

        @pl.loop(1, blocks - 1)
        def _(b):
            one_block(b, w)


def whiten(spectra, halves, edges, after):
    return pl.pallas_call(
        whiten_kernel,
        in_specs=[VMEM] * (5 + len(after)),
        out_specs=VMEM,
        out_shape=dtype_of(spectra.shape),
        compiler_params=params(),
        cost_estimate=pl.CostEstimate(flops=7 * spectra.size, bytes_accessed=2 * spectra.size, transcendentals=spectra.size // 2),
        name="whiten_windows",
    )(spectra, *halves, *edges, *after)


def merge_kernel(count, *refs):
    out_ref = refs[-1]
    at = 0
    for ref in refs[:count]:
        out_ref[at : at + ref.shape[0]] = ref[...]
        at += ref.shape[0]


def merge(blocks, done):
    return pl.pallas_call(
        functools.partial(merge_kernel, len(blocks)),
        in_specs=[VMEM] * (len(blocks) + len(done)),
        out_specs=VMEM,
        out_shape=dtype_of((sum(block.shape[0] for block in blocks),) + blocks[0].shape[1:]),
        compiler_params=params(),
        name="merge_rows",
    )(*blocks, *done)


def send(rows, bit):
    count = lax.axis_size("rx")
    return lax.ppermute(rows, "rx", [(i, i ^ bit) for i in range(count)])


def shifted(offsets, bit):
    return [offset ^ bit for offset in offsets]


def gather_rows(row, spectra, first, ends):
    count = lax.axis_size("rx")
    *far, near, across, core = [1 << k for k in reversed(range(count.bit_length() - 1))]
    rows, held = row, [0]
    for bit in far[:-1]:
        rows = merge([rows, send(rows, bit)], [])
        held = held + shifted(held, bit)
    far = far[-1]
    from_far = send(rows, far)
    edges = band_neighbours([end_amplitudes(end, rows) for end in ends])
    rows = merge([rows, from_far], [])
    held = held + shifted(held, far)
    others = [send(rows, bit) for bit in (near ^ across, across, near)]
    second = amplitudes(spectra, 1, rows)
    whitened = whiten(spectra, (first, second), edges, [rows])
    rows = merge([rows, *others], [whitened])
    held = held + shifted(held, near ^ across) + shifted(held, across) + shifted(held, near)
    return [rows, send(rows, core)], held + shifted(held, core), whitened


def cross_kernel(offsets, ends, *refs):
    *blocks, white_ref, out_ref, wide_ref, buffer, sem = refs
    sources = len(offsets)
    _, bins, width = blocks[0].shape
    windows = width // 2
    rank = lax.axis_index("rx")
    rows = [(ref, k) for ref in blocks for k in range(ref.shape[0])]
    pitch = wide_ref.shape[0] // sources
    for (ref, k), offset in zip(rows, offsets, strict=True):
        at = pl.multiple_of((rank ^ offset) * pitch, 8)
        wide_ref[pl.ds(at, bins)] = ref[k].astype(jnp.float32) * (1.0 / windows)
    sign = jnp.where(lax.broadcasted_iota(jnp.int32, (sources, width), 1) < windows, -1.0, 1.0)
    none = jnp.zeros((2 * sources, width), jnp.bfloat16)

    def left(f):
        first = wide_ref[pl.ds(f, sources, stride=pitch)]
        second = pltpu.roll(first, windows, 1) * sign
        return jnp.concatenate([first, second], 0).astype(jnp.bfloat16)

    def products(start, count):
        def scoped(*accumulators):
            for k, accumulator in enumerate(accumulators):
                f = start + 4 * k
                white = [jnp.concatenate([white_ref[0, f + j], white_ref[1, f + j]], 0) for j in range(4)]
                pairs = [jnp.concatenate(white[j : j + 2], 0) for j in (0, 2)]
                staged = (k // 2) % 2
                pltpu.matmul_push_rhs(jnp.concatenate(pairs, 1), staged, k % 2)
                rows = [jnp.concatenate([left(f + j), none] if j % 2 == 0 else [none, left(f + j)], 1) for j in range(4)]
                pltpu.matmul_acc_lhs(accumulator, jnp.concatenate(rows, 0), load_staged_rhs=staged)
            return [pltpu.matmul_pop(accumulator) for accumulator in accumulators]

        shape = (8 * sources, 2 * width)
        return pl.run_scoped(scoped, *[pltpu.ACC(k % 2)(shape, jnp.float32) for k in range(count // 4)])

    copies = []
    start = 0
    for end in ends:
        found = products(start, end - start)
        for f in range(start, end):
            j = (f - start) % 4
            columns = slice(j // 2 * width, (j // 2 + 1) * width)
            product = found[(f - start) // 4][2 * sources * j : 2 * sources * (j + 1), columns].astype(jnp.bfloat16)
            buffer[0, f] = product[:sources]
            buffer[1, f] = product[sources:]
        part = (slice(None), pl.ds(start, end - start))
        copy = pltpu.make_async_copy(buffer.at[part], out_ref.at[part], sem.at[len(copies)])
        copy.start()
        copies.append(copy)
        start = end
    for copy in copies:
        copy.wait()


def cross_spectra(blocks, offsets, whitened):
    sources = len(offsets)
    _, bins, width = blocks[0].shape
    channels = whitened.shape[-1]
    ends = [k * bins // 32 for k in (8, 16, 24, 28, 32)]
    shape = (2, bins, sources, channels)
    return pl.pallas_call(
        functools.partial(cross_kernel, offsets, ends),
        in_specs=[VMEM] * (len(blocks) + 1),
        out_specs=HBM,
        out_shape=dtype_of(shape),
        scratch_shapes=[
            pltpu.VMEM((sources * (bins + 8), width), jnp.float32),
            pltpu.VMEM(shape, jnp.bfloat16),
            pltpu.SemaphoreType.DMA((len(ends),)),
        ],
        compiler_params=params(),
        name="cross_spectra",
    )(*blocks, whitened)


def local(spectra, source_index):
    ends, columns, column = edge_amplitudes(
        pltpu.with_memory_space_constraint(spectra, pltpu.HBM),
        pltpu.with_memory_space_constraint(source_index, pltpu.HBM),
    )
    row, total = extract_row(spectra, column)
    first = amplitudes(spectra, 0, row)
    return cross_spectra(*gather_rows(whiten_row(row, total, columns, first), spectra, first, ends))


def solution(mesh):
    def placed(spectra, source_index):
        with jax.sharding.use_abstract_mesh(mesh.abstract_mesh):
            return body(spectra, source_index)

    body = jax.shard_map(
        local,
        mesh=mesh,
        in_specs=(P(None, "band", None, "rx"), P()),
        out_specs=P(None, "band", None, "rx"),
        check_vma=False,
    )
    return placed
```

```python
import functools

import jax
import jax.numpy as jnp
from jax import lax
from jax.experimental import pallas as pl
from jax.experimental.pallas import tpu as pltpu
from jax.sharding import PartitionSpec as P

HALF = 4
SPAN = 2 * HALF + 1
FLOOR = 0.1
TINY = 1e-37
MIB = 1024 * 1024
VMEM = pl.BlockSpec(memory_space=pltpu.VMEM)
SMEM = pl.BlockSpec(memory_space=pltpu.SMEM)
HBM = pl.BlockSpec(memory_space=pltpu.HBM)


def params(mib=24):
    return pltpu.CompilerParams(vmem_limit_bytes=mib * MIB)


def amplitude_of(power):
    return (power * lax.rsqrt(jnp.maximum(power, TINY))).astype(jnp.bfloat16)


def dtype_of(shape, dtype=jnp.bfloat16):
    return jax.ShapeDtypeStruct(shape, dtype)


def window_masks(windows):
    lane = lax.broadcasted_iota(jnp.int32, (windows, 2 * windows), 1)
    row = lax.broadcasted_iota(jnp.int32, (windows, 2 * windows), 0)
    return lane == row, lane == row + windows


def edge_kernel(index_ref, spectra_ref, *refs):
    *out_refs, column_ref, scalars, sem, index_sem = refs
    ends = len(out_refs) // 2
    bins, windows, channels = spectra_ref.shape[1:]
    index_copy = pltpu.make_async_copy(index_ref, scalars, index_sem)
    index_copy.start()
    if ends == 1:
        starts = [jnp.where(lax.axis_index("band") == 0, bins - HALF, 0)]
    else:
        starts = [bins - HALF, 0]
    copies = []
    for k, start in enumerate(starts):
        for part in range(2):
            for j in range(HALF):
                copy = pltpu.make_async_copy(spectra_ref.at[part, start + j], out_refs[k].at[part, j], sem.at[len(copies)])
                copy.start()
                copies.append(copy)
    index_copy.wait()
    rank = lax.axis_index("rx")
    column = jnp.full(column_ref.shape, scalars[rank] - rank * channels, jnp.int32)
    column_ref[...] = column
    masks = window_masks(windows)
    for k in range(ends):
        for copy in copies[2 * HALF * k : 2 * HALF * (k + 1)]:
            copy.wait()
        real = out_refs[k][0].astype(jnp.float32)
        imag = out_refs[k][1].astype(jnp.float32)
        amplitude = amplitude_of(real * real + imag * imag).astype(jnp.float32)
        pairs = []
        for first in range(0, HALF, 2):
            total = jnp.zeros((8, 2 * windows), jnp.float32)
            for w in range(0, windows, 8):
                for part, mask in enumerate(masks):
                    value = jnp.take_along_axis(amplitude[first + part, w : w + 8], column, axis=1, mode="promise_in_bounds")
                    total = jnp.where(mask[w : w + 8], value, total)
            pairs.append(total)
        total = jnp.concatenate(pairs, 1)
        out_refs[ends + k][...] = jnp.concatenate([total, total], 0).astype(jnp.bfloat16)


def edge_amplitudes(spectra, source_index):
    count = lax.axis_size("band")
    _, _, windows, channels = spectra.shape
    ends = 1 if count == 2 else 2
    *sent, column = pl.pallas_call(
        edge_kernel,
        in_specs=[HBM, HBM],
        out_specs=[VMEM] * (2 * ends + 1),
        out_shape=[dtype_of((2, HALF, windows, channels))] * ends + [dtype_of((16, HALF * windows))] * ends
        + [dtype_of((8, channels), jnp.int32)],
        scratch_shapes=[
            pltpu.SMEM(source_index.shape, source_index.dtype),
            pltpu.SemaphoreType.DMA((2 * HALF * ends,)),
            pltpu.SemaphoreType.DMA,
        ],
        compiler_params=params(),
        name="edge_amplitude",
    )(source_index, spectra)
    return sent[:ends], band_neighbours(sent[ends:]), column


def end_kernel(end_ref, after_ref, out_ref):
    real = end_ref[0].astype(jnp.float32)
    imag = end_ref[1].astype(jnp.float32)
    out_ref[...] = amplitude_of(real * real + imag * imag)


def end_amplitudes(end, after):
    return pl.pallas_call(
        end_kernel,
        in_specs=[VMEM] * 2,
        out_specs=VMEM,
        out_shape=dtype_of(end.shape[1:]),
        compiler_params=params(),
        name="end_amplitude",
    )(end, after)


def band_neighbours(ends):
    count = lax.axis_size("band")
    if count == 2:
        received = lax.ppermute(ends[0], "band", [(0, 1), (1, 0)])
        return received, received
    below = lax.ppermute(ends[0], "band", [(i, i + 1) for i in range(count - 1)])
    above = lax.ppermute(ends[1], "band", [(i + 1, i) for i in range(count - 1)])
    return below, above


def select_column(spectra_ref, column, staged, start, count, spread_ref):
    windows, channels = spectra_ref.shape[2:]
    masks = window_masks(windows)
    halves = count // 2

    def scoped(*accumulators):
        for k, accumulator in enumerate(accumulators):
            both = jnp.concatenate([spectra_ref[0, start + k], spectra_ref[1, start + k]], 1)
            pltpu.matmul_acc_lhs(accumulator, both, load_staged_rhs=0 if staged[k % 2] else None)
            staged[k % 2] = False
        return [pltpu.matmul_pop(accumulator) for accumulator in accumulators]

    found = pl.run_scoped(scoped, *[pltpu.ACC(k % 2)((windows, 256), jnp.float32) for k in range(halves)])
    for k in range(count):
        total = jnp.zeros((8, 2 * windows), jnp.float32)
        if k >= halves:
            values = [spectra_ref[part, start + k].astype(jnp.float32) for part in range(2)]
        for w in range(0, windows, 8):
            for part, mask in enumerate(masks):
                if k < halves:
                    value = found[k][w : w + 8, part * channels : (part + 1) * channels]
                else:
                    value = jnp.take_along_axis(values[part][w : w + 8], column, axis=1, mode="promise_in_bounds")
                total = jnp.where(mask[w : w + 8], value, total)
        spread_ref[(start + k) * 8 : (start + k + 1) * 8] = total


def extract_kernel(chunks, column_ref, spectra_ref, row_ref, total_ref, spread_ref, amplitude_ref):
    _, bins, windows, channels = spectra_ref.shape
    size = bins // chunks
    column = column_ref[...]
    wide = jnp.concatenate([column] * (256 // 8), 0)
    row = lax.broadcasted_iota(jnp.int32, (256, channels), 0)
    picks = jnp.concatenate([(row == wide + part * channels).astype(jnp.bfloat16) for part in range(2)], 1)
    for unit in range(2):
        pltpu.matmul_push_rhs(picks, 0, unit)
    staged = [True, True]
    group = min(64, size)
    for k in range(chunks):
        for start in range(k * size, (k + 1) * size, group):
            select_column(spectra_ref, column, staged, start, group, spread_ref)
            for f in range(start, start + group, 8):
                rows = [spread_ref[pl.ds(f * 8 + j, 8, stride=8)] for j in range(8)]
                row_ref[f : f + 8] = sum(rows[1:], rows[0])
    values = row_ref[...]
    squares = values * values
    amplitude = amplitude_of(squares + pltpu.roll(squares, windows, 1)).astype(jnp.float32)
    amplitude_ref[0:8] = jnp.zeros((8, 2 * windows), jnp.float32)
    amplitude_ref[8 : bins + 8] = amplitude
    amplitude_ref[bins + 8 : bins + 16] = jnp.zeros((8, 2 * windows), jnp.float32)
    total = amplitude
    for k in range(1, HALF + 1):
        total = total + (amplitude_ref[8 - k : bins + 8 - k] + amplitude_ref[8 + k : bins + 8 + k])
    total_ref[...] = total


def extract_row(spectra, column):
    _, bins, windows, _ = spectra.shape
    chunks = max(bins // 64, 1)
    return pl.pallas_call(
        functools.partial(extract_kernel, chunks),
        in_specs=[VMEM] * 2,
        out_specs=[VMEM] * 2,
        out_shape=[
            dtype_of((bins, 2 * windows), jnp.float32),
            dtype_of((bins, 2 * windows), jnp.float32),
        ],
        scratch_shapes=[pltpu.VMEM((8 * bins, 2 * windows), jnp.float32), pltpu.VMEM((bins + 16, 2 * windows), jnp.float32)],
        compiler_params=params(),
        cost_estimate=pl.CostEstimate(flops=0, bytes_accessed=4 * spectra.size, transcendentals=0),
        name="extract_row",
    )(column, spectra)


def whiten_row_kernel(row_ref, total_ref, below_ref, above_ref, after_ref, out_ref):
    bins, width = row_ref.shape
    windows = width // 2
    band, count = lax.axis_index("band"), lax.axis_size("band")
    below = jnp.sum(below_ref[...].astype(jnp.float32)[:8], 0, keepdims=True) * (band > 0).astype(jnp.float32)
    above = jnp.sum(above_ref[...].astype(jnp.float32)[:8], 0, keepdims=True) * (band < count - 1).astype(jnp.float32)
    sublane = lax.broadcasted_iota(jnp.int32, (8, windows), 0)
    low = jnp.zeros((8, windows), jnp.float32)
    high = jnp.zeros((8, windows), jnp.float32)
    for j in range(HALF):
        part = slice(j * windows, (j + 1) * windows)
        low = low + jnp.where(sublane <= j, below[:, part], 0.0)
        high = high + jnp.where(sublane >= 8 - HALF + j, above[:, part], 0.0)
    low = jnp.concatenate([low, low], 1)
    high = jnp.concatenate([high, high], 1)
    total = jnp.concatenate([total_ref[:8] + low, total_ref[8 : bins - 8], total_ref[bins - 8 :] + high], 0)
    out_ref[0] = (row_ref[...] / (total * (1.0 / SPAN) + FLOOR)).astype(jnp.bfloat16)


def whiten_row(row, total, columns, after):
    return pl.pallas_call(
        whiten_row_kernel,
        in_specs=[VMEM] * 5,
        out_specs=VMEM,
        out_shape=dtype_of((1,) + row.shape),
        compiler_params=params(),
        name="whiten_row",
    )(row, total, *columns, after)


def amplitude_kernel(first, spectra_ref, *refs):
    out_ref = refs[-1]
    bins = spectra_ref.shape[1]
    block = 16

    @pl.loop(0, bins // block)
    def _(b):
        at = pl.ds(b * block, block)
        for w in range(0, out_ref.shape[1], 16):
            window = slice(first + w, first + w + 16)
            real = spectra_ref[0, at, window].astype(jnp.float32)
            imag = spectra_ref[1, at, window].astype(jnp.float32)
            out_ref[at, w : w + 16] = amplitude_of(real * real + imag * imag).astype(jnp.float32)


def amplitudes(spectra, half, after):
    _, bins, windows, channels = spectra.shape
    share = spectra.size // 4
    return pl.pallas_call(
        functools.partial(amplitude_kernel, half * windows // 2),
        in_specs=[VMEM] * 2,
        out_specs=VMEM,
        out_shape=dtype_of((bins, windows // 2, channels), jnp.float32),
        compiler_params=params(),
        cost_estimate=pl.CostEstimate(flops=10 * share, bytes_accessed=4 * share, transcendentals=share),
        name="amplitude",
    )(spectra, after)


def whiten_kernel(spectra_ref, first_ref, second_ref, below_ref, above_ref, *refs):
    out_ref = refs[-1]
    _, bins, windows, _ = spectra_ref.shape
    band, count = lax.axis_index("band"), lax.axis_size("band")
    has_below = (band > 0).astype(jnp.float32)
    has_above = (band < count - 1).astype(jnp.float32)
    block = 16
    blocks = bins // block

    def one_block(b, w):
        at = b * block
        window = slice(w, w + 16)
        amplitude_ref, inner = (first_ref, w) if w < windows // 2 else (second_ref, w - windows // 2)
        one = []
        for k in range(-HALF, block + HALF):
            if isinstance(b, int) and at + k < 0:
                one.append(below_ref[HALF + k, window].astype(jnp.float32) * has_below)
            elif isinstance(b, int) and at + k >= bins:
                one.append(above_ref[at + k - bins, window].astype(jnp.float32) * has_above)
            else:
                one.append(amplitude_ref[at + k, inner : inner + 16])
        two = [one[k] + one[k + 1] for k in range(block + 2 * HALF - 1)]
        four = [two[k] + two[k + 2] for k in range(block + 2 * HALF - 3)]
        for k in range(block):
            total = (four[k] + four[k + 4]) + one[k + 8]
            scale = 1.0 / (total * (1.0 / SPAN) + FLOOR)
            for part in range(2):
                value = spectra_ref[part, at + k, window].astype(jnp.float32)
                out_ref[part, at + k, window] = (value * scale).astype(jnp.bfloat16)

    for w in range(0, windows, 16):
        one_block(0, w)
        one_block(blocks - 1, w)

        @pl.loop(1, blocks - 1)
        def _(b):
            one_block(b, w)


def whiten(spectra, halves, edges, after):
    return pl.pallas_call(
        whiten_kernel,
        in_specs=[VMEM] * (5 + len(after)),
        out_specs=VMEM,
        out_shape=dtype_of(spectra.shape),
        compiler_params=params(),
        cost_estimate=pl.CostEstimate(flops=7 * spectra.size, bytes_accessed=2 * spectra.size, transcendentals=spectra.size // 2),
        name="whiten_windows",
    )(spectra, *halves, *edges, *after)


def merge_kernel(count, *refs):
    out_ref = refs[-1]
    at = 0
    for ref in refs[:count]:
        out_ref[at : at + ref.shape[0]] = ref[...]
        at += ref.shape[0]


def merge(blocks, done):
    return pl.pallas_call(
        functools.partial(merge_kernel, len(blocks)),
        in_specs=[VMEM] * (len(blocks) + len(done)),
        out_specs=VMEM,
        out_shape=dtype_of((sum(block.shape[0] for block in blocks),) + blocks[0].shape[1:]),
        compiler_params=params(),
        name="merge_rows",
    )(*blocks, *done)


def send(rows, bit):
    count = lax.axis_size("rx")
    return lax.ppermute(rows, "rx", [(i, i ^ bit) for i in range(count)])


def shifted(offsets, bit):
    return [offset ^ bit for offset in offsets]


def gather_rows(row, spectra, first, ends):
    count = lax.axis_size("rx")
    *far, near, across, core = [1 << k for k in reversed(range(count.bit_length() - 1))]
    rows, held = row, [0]
    for bit in far[:-1]:
        rows = merge([rows, send(rows, bit)], [])
        held = held + shifted(held, bit)
    far = far[-1]
    from_far = send(rows, far)
    edges = band_neighbours([end_amplitudes(end, rows) for end in ends])
    rows = merge([rows, from_far], [])
    held = held + shifted(held, far)
    others = [send(rows, bit) for bit in (near ^ across, across, near)]
    second = amplitudes(spectra, 1, rows)
    whitened = whiten(spectra, (first, second), edges, [rows])
    rows = merge([rows, *others], [whitened])
    held = held + shifted(held, near ^ across) + shifted(held, across) + shifted(held, near)
    return [rows, send(rows, core)], held + shifted(held, core), whitened


def cross_kernel(offsets, ends, *refs):
    *blocks, white_ref, out_ref, wide_ref, buffer, sem = refs
    sources = len(offsets)
    _, bins, width = blocks[0].shape
    windows = width // 2
    rank = lax.axis_index("rx")
    rows = [(ref, k) for ref in blocks for k in range(ref.shape[0])]
    pitch = wide_ref.shape[0] // sources
    for (ref, k), offset in zip(rows, offsets, strict=True):
        at = pl.multiple_of((rank ^ offset) * pitch, 8)
        wide_ref[pl.ds(at, bins)] = ref[k].astype(jnp.float32) * (1.0 / windows)
    sign = jnp.where(lax.broadcasted_iota(jnp.int32, (sources, width), 1) < windows, -1.0, 1.0)
    none = jnp.zeros((2 * sources, width), jnp.bfloat16)

    def left(f):
        first = wide_ref[pl.ds(f, sources, stride=pitch)]
        second = pltpu.roll(first, windows, 1) * sign
        return jnp.concatenate([first, second], 0).astype(jnp.bfloat16)

    def products(start, count):
        def scoped(*accumulators):
            for k, accumulator in enumerate(accumulators):
                f = start + 4 * k
                white = [jnp.concatenate([white_ref[0, f + j], white_ref[1, f + j]], 0) for j in range(4)]
                pairs = [jnp.concatenate(white[j : j + 2], 0) for j in (0, 2)]
                staged = (k // 2) % 2
                pltpu.matmul_push_rhs(jnp.concatenate(pairs, 1), staged, k % 2)
                rows = [jnp.concatenate([left(f + j), none] if j % 2 == 0 else [none, left(f + j)], 1) for j in range(4)]
                pltpu.matmul_acc_lhs(accumulator, jnp.concatenate(rows, 0), load_staged_rhs=staged)
            return [pltpu.matmul_pop(accumulator) for accumulator in accumulators]

        shape = (8 * sources, 2 * width)
        return pl.run_scoped(scoped, *[pltpu.ACC(k % 2)(shape, jnp.float32) for k in range(count // 4)])

    copies = []
    start = 0
    for end in ends:
        found = products(start, end - start)
        for f in range(start, end):
            j = (f - start) % 4
            columns = slice(j // 2 * width, (j // 2 + 1) * width)
            product = found[(f - start) // 4][2 * sources * j : 2 * sources * (j + 1), columns].astype(jnp.bfloat16)
            buffer[0, f] = product[:sources]
            buffer[1, f] = product[sources:]
        part = (slice(None), pl.ds(start, end - start))
        copy = pltpu.make_async_copy(buffer.at[part], out_ref.at[part], sem.at[len(copies)])
        copy.start()
        copies.append(copy)
        start = end
    for copy in copies:
        copy.wait()


def cross_spectra(blocks, offsets, whitened):
    sources = len(offsets)
    _, bins, width = blocks[0].shape
    channels = whitened.shape[-1]
    ends = sorted({k * bins // 128 * 4 for k in (10, 20, 28, 31, 32)})
    shape = (2, bins, sources, channels)
    return pl.pallas_call(
        functools.partial(cross_kernel, offsets, ends),
        in_specs=[VMEM] * (len(blocks) + 1),
        out_specs=HBM,
        out_shape=dtype_of(shape),
        scratch_shapes=[
            pltpu.VMEM((sources * (bins + 8), width), jnp.float32),
            pltpu.VMEM(shape, jnp.bfloat16),
            pltpu.SemaphoreType.DMA((len(ends),)),
        ],
        compiler_params=params(),
        name="cross_spectra",
    )(*blocks, whitened)


def local(spectra, source_index):
    ends, columns, column = edge_amplitudes(
        pltpu.with_memory_space_constraint(spectra, pltpu.HBM),
        pltpu.with_memory_space_constraint(source_index, pltpu.HBM),
    )
    row, total = extract_row(spectra, column)
    first = amplitudes(spectra, 0, row)
    return cross_spectra(*gather_rows(whiten_row(row, total, columns, first), spectra, first, ends))


def solution(mesh):
    def placed(spectra, source_index):
        with jax.sharding.use_abstract_mesh(mesh.abstract_mesh):
            return body(spectra, source_index)

    body = jax.shard_map(
        local,
        mesh=mesh,
        in_specs=(P(None, "band", None, "rx"), P()),
        out_specs=P(None, "band", None, "rx"),
        check_vma=False,
    )
    return placed
```

```python
import functools

import jax
import jax.numpy as jnp
from jax import lax
from jax.experimental import pallas as pl
from jax.experimental.pallas import tpu as pltpu
from jax.sharding import PartitionSpec as P

HALF = 4
SPAN = 2 * HALF + 1
FLOOR = 0.1
TINY = 1e-37
MIB = 1024 * 1024
VMEM = pl.BlockSpec(memory_space=pltpu.VMEM)
SMEM = pl.BlockSpec(memory_space=pltpu.SMEM)
HBM = pl.BlockSpec(memory_space=pltpu.HBM)


def params(mib=24):
    return pltpu.CompilerParams(vmem_limit_bytes=mib * MIB)


def amplitude_of(power):
    return (power * lax.rsqrt(jnp.maximum(power, TINY))).astype(jnp.bfloat16)


def dtype_of(shape, dtype=jnp.bfloat16):
    return jax.ShapeDtypeStruct(shape, dtype)


def window_masks(windows):
    lane = lax.broadcasted_iota(jnp.int32, (windows, 2 * windows), 1)
    row = lax.broadcasted_iota(jnp.int32, (windows, 2 * windows), 0)
    return lane == row, lane == row + windows


def edge_kernel(index_ref, spectra_ref, *refs):
    *out_refs, column_ref, scalars, sem, index_sem = refs
    ends = len(out_refs) // 2
    bins, windows, channels = spectra_ref.shape[1:]
    index_copy = pltpu.make_async_copy(index_ref, scalars, index_sem)
    index_copy.start()
    if ends == 1:
        starts = [jnp.where(lax.axis_index("band") == 0, bins - HALF, 0)]
    else:
        starts = [bins - HALF, 0]
    copies = []
    for k, start in enumerate(starts):
        for part in range(2):
            for j in range(HALF):
                copy = pltpu.make_async_copy(spectra_ref.at[part, start + j], out_refs[k].at[part, j], sem.at[len(copies)])
                copy.start()
                copies.append(copy)
    index_copy.wait()
    rank = lax.axis_index("rx")
    column = jnp.full(column_ref.shape, scalars[rank] - rank * channels, jnp.int32)
    column_ref[...] = column
    masks = window_masks(windows)
    for k in range(ends):
        for copy in copies[2 * HALF * k : 2 * HALF * (k + 1)]:
            copy.wait()
        real = out_refs[k][0].astype(jnp.float32)
        imag = out_refs[k][1].astype(jnp.float32)
        amplitude = amplitude_of(real * real + imag * imag).astype(jnp.float32)
        pairs = []
        for first in range(0, HALF, 2):
            total = jnp.zeros((8, 2 * windows), jnp.float32)
            for w in range(0, windows, 8):
                for part, mask in enumerate(masks):
                    value = jnp.take_along_axis(amplitude[first + part, w : w + 8], column, axis=1, mode="promise_in_bounds")
                    total = jnp.where(mask[w : w + 8], value, total)
            pairs.append(total)
        total = jnp.concatenate(pairs, 1)
        out_refs[ends + k][...] = jnp.concatenate([total, total], 0).astype(jnp.bfloat16)


def edge_amplitudes(spectra, source_index):
    count = lax.axis_size("band")
    _, _, windows, channels = spectra.shape
    ends = 1 if count == 2 else 2
    *sent, column = pl.pallas_call(
        edge_kernel,
        in_specs=[HBM, HBM],
        out_specs=[VMEM] * (2 * ends + 1),
        out_shape=[dtype_of((2, HALF, windows, channels))] * ends + [dtype_of((16, HALF * windows))] * ends
        + [dtype_of((8, channels), jnp.int32)],
        scratch_shapes=[
            pltpu.SMEM(source_index.shape, source_index.dtype),
            pltpu.SemaphoreType.DMA((2 * HALF * ends,)),
            pltpu.SemaphoreType.DMA,
        ],
        compiler_params=params(),
        name="edge_amplitude",
    )(source_index, spectra)
    return sent[:ends], band_neighbours(sent[ends:]), column


def end_kernel(end_ref, after_ref, out_ref):
    real = end_ref[0].astype(jnp.float32)
    imag = end_ref[1].astype(jnp.float32)
    out_ref[...] = amplitude_of(real * real + imag * imag)


def end_amplitudes(end, after):
    return pl.pallas_call(
        end_kernel,
        in_specs=[VMEM] * 2,
        out_specs=VMEM,
        out_shape=dtype_of(end.shape[1:]),
        compiler_params=params(),
        name="end_amplitude",
    )(end, after)


def band_neighbours(ends):
    count = lax.axis_size("band")
    if count == 2:
        received = lax.ppermute(ends[0], "band", [(0, 1), (1, 0)])
        return received, received
    below = lax.ppermute(ends[0], "band", [(i, i + 1) for i in range(count - 1)])
    above = lax.ppermute(ends[1], "band", [(i + 1, i) for i in range(count - 1)])
    return below, above


def select_column(spectra_ref, column, staged, start, count, spread_ref):
    windows, channels = spectra_ref.shape[2:]
    masks = window_masks(windows)
    halves = count // 2

    def scoped(*accumulators):
        for k, accumulator in enumerate(accumulators):
            both = jnp.concatenate([spectra_ref[0, start + k], spectra_ref[1, start + k]], 1)
            pltpu.matmul_acc_lhs(accumulator, both, load_staged_rhs=0 if staged[k % 2] else None)
            staged[k % 2] = False
        return [pltpu.matmul_pop(accumulator) for accumulator in accumulators]

    found = pl.run_scoped(scoped, *[pltpu.ACC(k % 2)((windows, 256), jnp.float32) for k in range(halves)])
    for k in range(count):
        total = jnp.zeros((8, 2 * windows), jnp.float32)
        if k >= halves:
            values = [spectra_ref[part, start + k].astype(jnp.float32) for part in range(2)]
        for w in range(0, windows, 8):
            for part, mask in enumerate(masks):
                if k < halves:
                    value = found[k][w : w + 8, part * channels : (part + 1) * channels]
                else:
                    value = jnp.take_along_axis(values[part][w : w + 8], column, axis=1, mode="promise_in_bounds")
                total = jnp.where(mask[w : w + 8], value, total)
        spread_ref[(start + k) * 8 : (start + k + 1) * 8] = total


def extract_kernel(chunks, column_ref, spectra_ref, row_ref, total_ref, spread_ref, amplitude_ref):
    _, bins, windows, channels = spectra_ref.shape
    size = bins // chunks
    column = column_ref[...]
    wide = jnp.concatenate([column] * (256 // 8), 0)
    row = lax.broadcasted_iota(jnp.int32, (256, channels), 0)
    picks = jnp.concatenate([(row == wide + part * channels).astype(jnp.bfloat16) for part in range(2)], 1)
    for unit in range(2):
        pltpu.matmul_push_rhs(picks, 0, unit)
    staged = [True, True]
    group = min(64, size)
    for k in range(chunks):
        for start in range(k * size, (k + 1) * size, group):
            select_column(spectra_ref, column, staged, start, group, spread_ref)
            for f in range(start, start + group, 8):
                rows = [spread_ref[pl.ds(f * 8 + j, 8, stride=8)] for j in range(8)]
                row_ref[f : f + 8] = sum(rows[1:], rows[0])
    values = row_ref[...]
    squares = values * values
    amplitude = amplitude_of(squares + pltpu.roll(squares, windows, 1)).astype(jnp.float32)
    amplitude_ref[0:8] = jnp.zeros((8, 2 * windows), jnp.float32)
    amplitude_ref[8 : bins + 8] = amplitude
    amplitude_ref[bins + 8 : bins + 16] = jnp.zeros((8, 2 * windows), jnp.float32)
    total = amplitude
    for k in range(1, HALF + 1):
        total = total + (amplitude_ref[8 - k : bins + 8 - k] + amplitude_ref[8 + k : bins + 8 + k])
    total_ref[...] = total


def extract_row(spectra, column):
    _, bins, windows, _ = spectra.shape
    chunks = max(bins // 64, 1)
    return pl.pallas_call(
        functools.partial(extract_kernel, chunks),
        in_specs=[VMEM] * 2,
        out_specs=[VMEM] * 2,
        out_shape=[
            dtype_of((bins, 2 * windows), jnp.float32),
            dtype_of((bins, 2 * windows), jnp.float32),
        ],
        scratch_shapes=[pltpu.VMEM((8 * bins, 2 * windows), jnp.float32), pltpu.VMEM((bins + 16, 2 * windows), jnp.float32)],
        compiler_params=params(),
        cost_estimate=pl.CostEstimate(flops=0, bytes_accessed=4 * spectra.size, transcendentals=0),
        name="extract_row",
    )(column, spectra)


def whiten_row_kernel(row_ref, total_ref, below_ref, above_ref, after_ref, out_ref):
    bins, width = row_ref.shape
    windows = width // 2
    band, count = lax.axis_index("band"), lax.axis_size("band")
    below = jnp.sum(below_ref[...].astype(jnp.float32)[:8], 0, keepdims=True) * (band > 0).astype(jnp.float32)
    above = jnp.sum(above_ref[...].astype(jnp.float32)[:8], 0, keepdims=True) * (band < count - 1).astype(jnp.float32)
    sublane = lax.broadcasted_iota(jnp.int32, (8, windows), 0)
    low = jnp.zeros((8, windows), jnp.float32)
    high = jnp.zeros((8, windows), jnp.float32)
    for j in range(HALF):
        part = slice(j * windows, (j + 1) * windows)
        low = low + jnp.where(sublane <= j, below[:, part], 0.0)
        high = high + jnp.where(sublane >= 8 - HALF + j, above[:, part], 0.0)
    low = jnp.concatenate([low, low], 1)
    high = jnp.concatenate([high, high], 1)
    total = jnp.concatenate([total_ref[:8] + low, total_ref[8 : bins - 8], total_ref[bins - 8 :] + high], 0)
    out_ref[0] = (row_ref[...] / (total * (1.0 / SPAN) + FLOOR)).astype(jnp.bfloat16)


def whiten_row(row, total, columns, after):
    return pl.pallas_call(
        whiten_row_kernel,
        in_specs=[VMEM] * 5,
        out_specs=VMEM,
        out_shape=dtype_of((1,) + row.shape),
        compiler_params=params(),
        name="whiten_row",
    )(row, total, *columns, after)


def amplitude_kernel(first, spectra_ref, *refs):
    out_ref = refs[-1]
    bins = spectra_ref.shape[1]
    block = 16

    @pl.loop(0, bins // block)
    def _(b):
        at = pl.ds(b * block, block)
        for w in range(0, out_ref.shape[1], 16):
            window = slice(first + w, first + w + 16)
            real = spectra_ref[0, at, window].astype(jnp.float32)
            imag = spectra_ref[1, at, window].astype(jnp.float32)
            out_ref[at, w : w + 16] = amplitude_of(real * real + imag * imag).astype(jnp.float32)


def amplitudes(spectra, half, after):
    _, bins, windows, channels = spectra.shape
    share = spectra.size // 4
    return pl.pallas_call(
        functools.partial(amplitude_kernel, half * windows // 2),
        in_specs=[VMEM] * 2,
        out_specs=VMEM,
        out_shape=dtype_of((bins, windows // 2, channels), jnp.float32),
        compiler_params=params(),
        cost_estimate=pl.CostEstimate(flops=10 * share, bytes_accessed=4 * share, transcendentals=share),
        name="amplitude",
    )(spectra, after)


def whiten_kernel(spectra_ref, first_ref, second_ref, below_ref, above_ref, *refs):
    out_ref = refs[-1]
    _, bins, windows, _ = spectra_ref.shape
    band, count = lax.axis_index("band"), lax.axis_size("band")
    has_below = (band > 0).astype(jnp.float32)
    has_above = (band < count - 1).astype(jnp.float32)
    block = 16
    blocks = bins // block

    def one_block(b, w):
        at = b * block
        window = slice(w, w + 16)
        amplitude_ref, inner = (first_ref, w) if w < windows // 2 else (second_ref, w - windows // 2)
        one = []
        for k in range(-HALF, block + HALF):
            if isinstance(b, int) and at + k < 0:
                one.append(below_ref[HALF + k, window].astype(jnp.float32) * has_below)
            elif isinstance(b, int) and at + k >= bins:
                one.append(above_ref[at + k - bins, window].astype(jnp.float32) * has_above)
            else:
                one.append(amplitude_ref[at + k, inner : inner + 16])
        two = [one[k] + one[k + 1] for k in range(block + 2 * HALF - 1)]
        four = [two[k] + two[k + 2] for k in range(block + 2 * HALF - 3)]
        for k in range(block):
            total = (four[k] + four[k + 4]) + one[k + 8]
            scale = 1.0 / (total * (1.0 / SPAN) + FLOOR)
            for part in range(2):
                value = spectra_ref[part, at + k, window].astype(jnp.float32)
                out_ref[part, at + k, window] = (value * scale).astype(jnp.bfloat16)

    for w in range(0, windows, 16):
        one_block(0, w)
        one_block(blocks - 1, w)

        @pl.loop(1, blocks - 1)
        def _(b):
            one_block(b, w)


def whiten(spectra, halves, edges, after):
    return pl.pallas_call(
        whiten_kernel,
        in_specs=[VMEM] * (5 + len(after)),
        out_specs=VMEM,
        out_shape=dtype_of(spectra.shape),
        compiler_params=params(),
        cost_estimate=pl.CostEstimate(flops=7 * spectra.size, bytes_accessed=2 * spectra.size, transcendentals=spectra.size // 2),
        name="whiten_windows",
    )(spectra, *halves, *edges, *after)


def merge_kernel(count, *refs):
    out_ref = refs[-1]
    at = 0
    for ref in refs[:count]:
        out_ref[at : at + ref.shape[0]] = ref[...]
        at += ref.shape[0]


def merge(blocks, done):
    return pl.pallas_call(
        functools.partial(merge_kernel, len(blocks)),
        in_specs=[VMEM] * (len(blocks) + len(done)),
        out_specs=VMEM,
        out_shape=dtype_of((sum(block.shape[0] for block in blocks),) + blocks[0].shape[1:]),
        compiler_params=params(),
        name="merge_rows",
    )(*blocks, *done)


def send(rows, bit):
    count = lax.axis_size("rx")
    return lax.ppermute(rows, "rx", [(i, i ^ bit) for i in range(count)])


def shifted(offsets, bit):
    return [offset ^ bit for offset in offsets]


def gather_rows(row, spectra, first, ends):
    count = lax.axis_size("rx")
    *far, near, across, core = [1 << k for k in reversed(range(count.bit_length() - 1))]
    rows, held = row, [0]
    for bit in far[:-1]:
        rows = merge([rows, send(rows, bit)], [])
        held = held + shifted(held, bit)
    far = far[-1]
    from_far = send(rows, far)
    edges = band_neighbours([end_amplitudes(end, rows) for end in ends])
    rows = merge([rows, from_far], [])
    held = held + shifted(held, far)
    others = [send(rows, bit) for bit in (near ^ across, near, across)]
    second = amplitudes(spectra, 1, rows)
    whitened = whiten(spectra, (first, second), edges, [rows])
    rows = merge([rows, *others], [whitened])
    held = held + shifted(held, near ^ across) + shifted(held, near) + shifted(held, across)
    return [rows, send(rows, core)], held + shifted(held, core), whitened


def cross_kernel(offsets, ends, *refs):
    *blocks, white_ref, out_ref, wide_ref, buffer, sem = refs
    sources = len(offsets)
    _, bins, width = blocks[0].shape
    windows = width // 2
    rank = lax.axis_index("rx")
    rows = [(ref, k) for ref in blocks for k in range(ref.shape[0])]
    pitch = wide_ref.shape[0] // sources
    for (ref, k), offset in zip(rows, offsets, strict=True):
        at = pl.multiple_of((rank ^ offset) * pitch, 8)
        wide_ref[pl.ds(at, bins)] = ref[k].astype(jnp.float32) * (1.0 / windows)
    sign = jnp.where(lax.broadcasted_iota(jnp.int32, (sources, width), 1) < windows, -1.0, 1.0)
    none = jnp.zeros((2 * sources, width), jnp.bfloat16)

    def left(f):
        first = wide_ref[pl.ds(f, sources, stride=pitch)]
        second = pltpu.roll(first, windows, 1) * sign
        return jnp.concatenate([first, second], 0).astype(jnp.bfloat16)

    def products(start, count):
        def scoped(*accumulators):
            for k, accumulator in enumerate(accumulators):
                f = start + 4 * k
                white = [jnp.concatenate([white_ref[0, f + j], white_ref[1, f + j]], 0) for j in range(4)]
                pairs = [jnp.concatenate(white[j : j + 2], 0) for j in (0, 2)]
                staged = (k // 2) % 2
                pltpu.matmul_push_rhs(jnp.concatenate(pairs, 1), staged, k % 2)
                rows = [jnp.concatenate([left(f + j), none] if j % 2 == 0 else [none, left(f + j)], 1) for j in range(4)]
                pltpu.matmul_acc_lhs(accumulator, jnp.concatenate(rows, 0), load_staged_rhs=staged)
            return [pltpu.matmul_pop(accumulator) for accumulator in accumulators]

        shape = (8 * sources, 2 * width)
        return pl.run_scoped(scoped, *[pltpu.ACC(k % 2)(shape, jnp.float32) for k in range(count // 4)])

    copies = []
    start = 0
    for end in ends:
        found = products(start, end - start)
        for f in range(start, end):
            j = (f - start) % 4
            columns = slice(j // 2 * width, (j // 2 + 1) * width)
            product = found[(f - start) // 4][2 * sources * j : 2 * sources * (j + 1), columns].astype(jnp.bfloat16)
            buffer[0, f] = product[:sources]
            buffer[1, f] = product[sources:]
        part = (slice(None), pl.ds(start, end - start))
        copy = pltpu.make_async_copy(buffer.at[part], out_ref.at[part], sem.at[len(copies)])
        copy.start()
        copies.append(copy)
        start = end
    for copy in copies:
        copy.wait()


def cross_spectra(blocks, offsets, whitened):
    sources = len(offsets)
    _, bins, width = blocks[0].shape
    channels = whitened.shape[-1]
    ends = sorted({k * bins // 128 * 4 for k in (10, 20, 28, 31, 32)})
    shape = (2, bins, sources, channels)
    return pl.pallas_call(
        functools.partial(cross_kernel, offsets, ends),
        in_specs=[VMEM] * (len(blocks) + 1),
        out_specs=HBM,
        out_shape=dtype_of(shape),
        scratch_shapes=[
            pltpu.VMEM((sources * (bins + 8), width), jnp.float32),
            pltpu.VMEM(shape, jnp.bfloat16),
            pltpu.SemaphoreType.DMA((len(ends),)),
        ],
        compiler_params=params(),
        name="cross_spectra",
    )(*blocks, whitened)


def local(spectra, source_index):
    ends, columns, column = edge_amplitudes(
        pltpu.with_memory_space_constraint(spectra, pltpu.HBM),
        pltpu.with_memory_space_constraint(source_index, pltpu.HBM),
    )
    row, total = extract_row(spectra, column)
    first = amplitudes(spectra, 0, row)
    return cross_spectra(*gather_rows(whiten_row(row, total, columns, first), spectra, first, ends))


def solution(mesh):
    def placed(spectra, source_index):
        with jax.sharding.use_abstract_mesh(mesh.abstract_mesh):
            return body(spectra, source_index)

    body = jax.shard_map(
        local,
        mesh=mesh,
        in_specs=(P(None, "band", None, "rx"), P()),
        out_specs=P(None, "band", None, "rx"),
        check_vma=False,
    )
    return placed
```

```python
import functools

import jax
import jax.numpy as jnp
from jax import lax
from jax.experimental import pallas as pl
from jax.experimental.pallas import tpu as pltpu
from jax.sharding import PartitionSpec as P

HALF = 4
SPAN = 2 * HALF + 1
FLOOR = 0.1
TINY = 1e-37
MIB = 1024 * 1024
VMEM = pl.BlockSpec(memory_space=pltpu.VMEM)
SMEM = pl.BlockSpec(memory_space=pltpu.SMEM)
HBM = pl.BlockSpec(memory_space=pltpu.HBM)


def params(mib=24):
    return pltpu.CompilerParams(vmem_limit_bytes=mib * MIB)


def amplitude_of(power):
    return (power * lax.rsqrt(jnp.maximum(power, TINY))).astype(jnp.bfloat16)


def dtype_of(shape, dtype=jnp.bfloat16):
    return jax.ShapeDtypeStruct(shape, dtype)


def window_masks(windows):
    lane = lax.broadcasted_iota(jnp.int32, (windows, 2 * windows), 1)
    row = lax.broadcasted_iota(jnp.int32, (windows, 2 * windows), 0)
    return lane == row, lane == row + windows


def edge_kernel(index_ref, spectra_ref, *refs):
    *out_refs, column_ref, scalars, sem, index_sem = refs
    ends = len(out_refs) // 2
    bins, windows, channels = spectra_ref.shape[1:]
    index_copy = pltpu.make_async_copy(index_ref, scalars, index_sem)
    index_copy.start()
    if ends == 1:
        starts = [jnp.where(lax.axis_index("band") == 0, bins - HALF, 0)]
    else:
        starts = [bins - HALF, 0]
    copies = []
    for k, start in enumerate(starts):
        for part in range(2):
            for j in range(HALF):
                copy = pltpu.make_async_copy(spectra_ref.at[part, start + j], out_refs[k].at[part, j], sem.at[len(copies)])
                copy.start()
                copies.append(copy)
    masks = window_masks(windows)
    column = None
    for k in range(ends):
        for copy in copies[2 * HALF * k : 2 * HALF * (k + 1)]:
            copy.wait()
        real = out_refs[k][0].astype(jnp.float32)
        imag = out_refs[k][1].astype(jnp.float32)
        amplitude = amplitude_of(real * real + imag * imag).astype(jnp.float32)
        if column is None:
            index_copy.wait()
            rank = lax.axis_index("rx")
            column = jnp.full(column_ref.shape, scalars[rank] - rank * channels, jnp.int32)
            column_ref[...] = column
        pairs = []
        for first in range(0, HALF, 2):
            total = jnp.zeros((8, 2 * windows), jnp.float32)
            for w in range(0, windows, 8):
                for part, mask in enumerate(masks):
                    value = jnp.take_along_axis(amplitude[first + part, w : w + 8], column, axis=1, mode="promise_in_bounds")
                    total = jnp.where(mask[w : w + 8], value, total)
            pairs.append(total)
        total = jnp.concatenate(pairs, 1)
        out_refs[ends + k][...] = jnp.concatenate([total, total], 0).astype(jnp.bfloat16)


def edge_amplitudes(spectra, source_index):
    count = lax.axis_size("band")
    _, _, windows, channels = spectra.shape
    ends = 1 if count == 2 else 2
    *sent, column = pl.pallas_call(
        edge_kernel,
        in_specs=[HBM, HBM],
        out_specs=[VMEM] * (2 * ends + 1),
        out_shape=[dtype_of((2, HALF, windows, channels))] * ends + [dtype_of((16, HALF * windows))] * ends
        + [dtype_of((8, channels), jnp.int32)],
        scratch_shapes=[
            pltpu.SMEM(source_index.shape, source_index.dtype),
            pltpu.SemaphoreType.DMA((2 * HALF * ends,)),
            pltpu.SemaphoreType.DMA,
        ],
        compiler_params=params(),
        name="edge_amplitude",
    )(source_index, spectra)
    return sent[:ends], band_neighbours(sent[ends:]), column


def end_kernel(end_ref, after_ref, out_ref):
    real = end_ref[0].astype(jnp.float32)
    imag = end_ref[1].astype(jnp.float32)
    out_ref[...] = amplitude_of(real * real + imag * imag)


def end_amplitudes(end, after):
    return pl.pallas_call(
        end_kernel,
        in_specs=[VMEM] * 2,
        out_specs=VMEM,
        out_shape=dtype_of(end.shape[1:]),
        compiler_params=params(),
        name="end_amplitude",
    )(end, after)


def band_neighbours(ends):
    count = lax.axis_size("band")
    if count == 2:
        received = lax.ppermute(ends[0], "band", [(0, 1), (1, 0)])
        return received, received
    below = lax.ppermute(ends[0], "band", [(i, i + 1) for i in range(count - 1)])
    above = lax.ppermute(ends[1], "band", [(i + 1, i) for i in range(count - 1)])
    return below, above


def select_column(spectra_ref, column, staged, start, count, spread_ref):
    windows, channels = spectra_ref.shape[2:]
    masks = window_masks(windows)
    halves = count // 2

    def scoped(*accumulators):
        for k, accumulator in enumerate(accumulators):
            both = jnp.concatenate([spectra_ref[0, start + k], spectra_ref[1, start + k]], 1)
            pltpu.matmul_acc_lhs(accumulator, both, load_staged_rhs=0 if staged[k % 2] else None)
            staged[k % 2] = False
        return [pltpu.matmul_pop(accumulator) for accumulator in accumulators]

    found = pl.run_scoped(scoped, *[pltpu.ACC(k % 2)((windows, 256), jnp.float32) for k in range(halves)])
    for k in range(count):
        total = jnp.zeros((8, 2 * windows), jnp.float32)
        if k >= halves:
            values = [spectra_ref[part, start + k].astype(jnp.float32) for part in range(2)]
        for w in range(0, windows, 8):
            for part, mask in enumerate(masks):
                if k < halves:
                    value = found[k][w : w + 8, part * channels : (part + 1) * channels]
                else:
                    value = jnp.take_along_axis(values[part][w : w + 8], column, axis=1, mode="promise_in_bounds")
                total = jnp.where(mask[w : w + 8], value, total)
        spread_ref[(start + k) * 8 : (start + k + 1) * 8] = total


def extract_kernel(chunks, column_ref, spectra_ref, row_ref, total_ref, spread_ref, amplitude_ref):
    _, bins, windows, channels = spectra_ref.shape
    size = bins // chunks
    column = column_ref[...]
    wide = jnp.concatenate([column] * (256 // 8), 0)
    row = lax.broadcasted_iota(jnp.int32, (256, channels), 0)
    picks = jnp.concatenate([(row == wide + part * channels).astype(jnp.bfloat16) for part in range(2)], 1)
    for unit in range(2):
        pltpu.matmul_push_rhs(picks, 0, unit)
    staged = [True, True]
    group = min(64, size)
    for k in range(chunks):
        for start in range(k * size, (k + 1) * size, group):
            select_column(spectra_ref, column, staged, start, group, spread_ref)
            for f in range(start, start + group, 8):
                rows = [spread_ref[pl.ds(f * 8 + j, 8, stride=8)] for j in range(8)]
                row_ref[f : f + 8] = sum(rows[1:], rows[0])
    values = row_ref[...]
    squares = values * values
    amplitude = amplitude_of(squares + pltpu.roll(squares, windows, 1)).astype(jnp.float32)
    amplitude_ref[0:8] = jnp.zeros((8, 2 * windows), jnp.float32)
    amplitude_ref[8 : bins + 8] = amplitude
    amplitude_ref[bins + 8 : bins + 16] = jnp.zeros((8, 2 * windows), jnp.float32)
    total = amplitude
    for k in range(1, HALF + 1):
        total = total + (amplitude_ref[8 - k : bins + 8 - k] + amplitude_ref[8 + k : bins + 8 + k])
    total_ref[...] = total


def extract_row(spectra, column):
    _, bins, windows, _ = spectra.shape
    chunks = max(bins // 64, 1)
    return pl.pallas_call(
        functools.partial(extract_kernel, chunks),
        in_specs=[VMEM] * 2,
        out_specs=[VMEM] * 2,
        out_shape=[
            dtype_of((bins, 2 * windows), jnp.float32),
            dtype_of((bins, 2 * windows), jnp.float32),
        ],
        scratch_shapes=[pltpu.VMEM((8 * bins, 2 * windows), jnp.float32), pltpu.VMEM((bins + 16, 2 * windows), jnp.float32)],
        compiler_params=params(),
        cost_estimate=pl.CostEstimate(flops=0, bytes_accessed=4 * spectra.size, transcendentals=0),
        name="extract_row",
    )(column, spectra)


def whiten_row_kernel(row_ref, total_ref, below_ref, above_ref, after_ref, out_ref):
    bins, width = row_ref.shape
    windows = width // 2
    band, count = lax.axis_index("band"), lax.axis_size("band")
    below = jnp.sum(below_ref[...].astype(jnp.float32)[:8], 0, keepdims=True) * (band > 0).astype(jnp.float32)
    above = jnp.sum(above_ref[...].astype(jnp.float32)[:8], 0, keepdims=True) * (band < count - 1).astype(jnp.float32)
    sublane = lax.broadcasted_iota(jnp.int32, (8, windows), 0)
    low = jnp.zeros((8, windows), jnp.float32)
    high = jnp.zeros((8, windows), jnp.float32)
    for j in range(HALF):
        part = slice(j * windows, (j + 1) * windows)
        low = low + jnp.where(sublane <= j, below[:, part], 0.0)
        high = high + jnp.where(sublane >= 8 - HALF + j, above[:, part], 0.0)
    low = jnp.concatenate([low, low], 1)
    high = jnp.concatenate([high, high], 1)
    total = jnp.concatenate([total_ref[:8] + low, total_ref[8 : bins - 8], total_ref[bins - 8 :] + high], 0)
    out_ref[0] = (row_ref[...] / (total * (1.0 / SPAN) + FLOOR)).astype(jnp.bfloat16)


def whiten_row(row, total, columns, after):
    return pl.pallas_call(
        whiten_row_kernel,
        in_specs=[VMEM] * 5,
        out_specs=VMEM,
        out_shape=dtype_of((1,) + row.shape),
        compiler_params=params(),
        name="whiten_row",
    )(row, total, *columns, after)


def amplitude_kernel(first, spectra_ref, *refs):
    out_ref = refs[-1]
    bins = spectra_ref.shape[1]
    block = 16

    @pl.loop(0, bins // block)
    def _(b):
        at = pl.ds(b * block, block)
        for w in range(0, out_ref.shape[1], 16):
            window = slice(first + w, first + w + 16)
            real = spectra_ref[0, at, window].astype(jnp.float32)
            imag = spectra_ref[1, at, window].astype(jnp.float32)
            out_ref[at, w : w + 16] = amplitude_of(real * real + imag * imag).astype(jnp.float32)


def amplitudes(spectra, half, after):
    _, bins, windows, channels = spectra.shape
    share = spectra.size // 4
    return pl.pallas_call(
        functools.partial(amplitude_kernel, half * windows // 2),
        in_specs=[VMEM] * 2,
        out_specs=VMEM,
        out_shape=dtype_of((bins, windows // 2, channels), jnp.float32),
        compiler_params=params(),
        cost_estimate=pl.CostEstimate(flops=10 * share, bytes_accessed=4 * share, transcendentals=share),
        name="amplitude",
    )(spectra, after)


def whiten_kernel(spectra_ref, first_ref, second_ref, below_ref, above_ref, *refs):
    out_ref = refs[-1]
    _, bins, windows, _ = spectra_ref.shape
    band, count = lax.axis_index("band"), lax.axis_size("band")
    has_below = (band > 0).astype(jnp.float32)
    has_above = (band < count - 1).astype(jnp.float32)
    block = 16
    blocks = bins // block

    def one_block(b, w):
        at = b * block
        window = slice(w, w + 16)
        amplitude_ref, inner = (first_ref, w) if w < windows // 2 else (second_ref, w - windows // 2)
        one = []
        for k in range(-HALF, block + HALF):
            if isinstance(b, int) and at + k < 0:
                one.append(below_ref[HALF + k, window].astype(jnp.float32) * has_below)
            elif isinstance(b, int) and at + k >= bins:
                one.append(above_ref[at + k - bins, window].astype(jnp.float32) * has_above)
            else:
                one.append(amplitude_ref[at + k, inner : inner + 16])
        two = [one[k] + one[k + 1] for k in range(block + 2 * HALF - 1)]
        four = [two[k] + two[k + 2] for k in range(block + 2 * HALF - 3)]
        for k in range(block):
            total = (four[k] + four[k + 4]) + one[k + 8]
            scale = 1.0 / (total * (1.0 / SPAN) + FLOOR)
            for part in range(2):
                value = spectra_ref[part, at + k, window].astype(jnp.float32)
                out_ref[part, at + k, window] = (value * scale).astype(jnp.bfloat16)

    for w in range(0, windows, 16):
        one_block(0, w)
        one_block(blocks - 1, w)

        @pl.loop(1, blocks - 1)
        def _(b):
            one_block(b, w)


def whiten(spectra, halves, edges, after):
    return pl.pallas_call(
        whiten_kernel,
        in_specs=[VMEM] * (5 + len(after)),
        out_specs=VMEM,
        out_shape=dtype_of(spectra.shape),
        compiler_params=params(),
        cost_estimate=pl.CostEstimate(flops=7 * spectra.size, bytes_accessed=2 * spectra.size, transcendentals=spectra.size // 2),
        name="whiten_windows",
    )(spectra, *halves, *edges, *after)


def merge_kernel(count, *refs):
    out_ref = refs[-1]
    at = 0
    for ref in refs[:count]:
        out_ref[at : at + ref.shape[0]] = ref[...]
        at += ref.shape[0]


def merge(blocks, done):
    return pl.pallas_call(
        functools.partial(merge_kernel, len(blocks)),
        in_specs=[VMEM] * (len(blocks) + len(done)),
        out_specs=VMEM,
        out_shape=dtype_of((sum(block.shape[0] for block in blocks),) + blocks[0].shape[1:]),
        compiler_params=params(),
        name="merge_rows",
    )(*blocks, *done)


def send(rows, bit):
    count = lax.axis_size("rx")
    return lax.ppermute(rows, "rx", [(i, i ^ bit) for i in range(count)])


def shifted(offsets, bit):
    return [offset ^ bit for offset in offsets]


def gather_rows(row, spectra, first, ends):
    count = lax.axis_size("rx")
    *far, near, across, core = [1 << k for k in reversed(range(count.bit_length() - 1))]
    rows, held = row, [0]
    for bit in far[:-1]:
        rows = merge([rows, send(rows, bit)], [])
        held = held + shifted(held, bit)
    far = far[-1]
    from_far = send(rows, far)
    edges = band_neighbours([end_amplitudes(end, rows) for end in ends])
    rows = merge([rows, from_far], [])
    held = held + shifted(held, far)
    others = [send(rows, bit) for bit in (near ^ across, across, near)]
    second = amplitudes(spectra, 1, rows)
    whitened = whiten(spectra, (first, second), edges, [rows])
    rows = merge([rows, *others], [whitened])
    held = held + shifted(held, near ^ across) + shifted(held, across) + shifted(held, near)
    return [rows, send(rows, core)], held + shifted(held, core), whitened


def cross_kernel(offsets, ends, *refs):
    *blocks, white_ref, out_ref, wide_ref, buffer, sem = refs
    sources = len(offsets)
    _, bins, width = blocks[0].shape
    windows = width // 2
    rank = lax.axis_index("rx")
    rows = [(ref, k) for ref in blocks for k in range(ref.shape[0])]
    pitch = wide_ref.shape[0] // sources
    for (ref, k), offset in zip(rows, offsets, strict=True):
        at = pl.multiple_of((rank ^ offset) * pitch, 8)
        wide_ref[pl.ds(at, bins)] = ref[k].astype(jnp.float32) * (1.0 / windows)
    sign = jnp.where(lax.broadcasted_iota(jnp.int32, (sources, width), 1) < windows, -1.0, 1.0)
    none = jnp.zeros((2 * sources, width), jnp.bfloat16)

    def left(f):
        first = wide_ref[pl.ds(f, sources, stride=pitch)]
        second = pltpu.roll(first, windows, 1) * sign
        return jnp.concatenate([first, second], 0).astype(jnp.bfloat16)

    def products(start, count):
        def scoped(*accumulators):
            for k, accumulator in enumerate(accumulators):
                f = start + 4 * k
                white = [jnp.concatenate([white_ref[0, f + j], white_ref[1, f + j]], 0) for j in range(4)]
                pairs = [jnp.concatenate(white[j : j + 2], 0) for j in (0, 2)]
                staged = (k // 2) % 2
                pltpu.matmul_push_rhs(jnp.concatenate(pairs, 1), staged, k % 2)
                rows = [jnp.concatenate([left(f + j), none] if j % 2 == 0 else [none, left(f + j)], 1) for j in range(4)]
                pltpu.matmul_acc_lhs(accumulator, jnp.concatenate(rows, 0), load_staged_rhs=staged)
            return [pltpu.matmul_pop(accumulator) for accumulator in accumulators]

        shape = (8 * sources, 2 * width)
        return pl.run_scoped(scoped, *[pltpu.ACC(k % 2)(shape, jnp.float32) for k in range(count // 4)])

    copies = []
    start = 0
    for end in ends:
        found = products(start, end - start)
        for f in range(start, end):
            j = (f - start) % 4
            columns = slice(j // 2 * width, (j // 2 + 1) * width)
            product = found[(f - start) // 4][2 * sources * j : 2 * sources * (j + 1), columns].astype(jnp.bfloat16)
            buffer[0, f] = product[:sources]
            buffer[1, f] = product[sources:]
        part = (slice(None), pl.ds(start, end - start))
        copy = pltpu.make_async_copy(buffer.at[part], out_ref.at[part], sem.at[len(copies)])
        copy.start()
        copies.append(copy)
        start = end
    for copy in copies:
        copy.wait()


def cross_spectra(blocks, offsets, whitened):
    sources = len(offsets)
    _, bins, width = blocks[0].shape
    channels = whitened.shape[-1]
    ends = sorted({k * bins // 128 * 4 for k in (10, 20, 28, 31, 32)})
    shape = (2, bins, sources, channels)
    return pl.pallas_call(
        functools.partial(cross_kernel, offsets, ends),
        in_specs=[VMEM] * (len(blocks) + 1),
        out_specs=HBM,
        out_shape=dtype_of(shape),
        scratch_shapes=[
            pltpu.VMEM((sources * (bins + 8), width), jnp.float32),
            pltpu.VMEM(shape, jnp.bfloat16),
            pltpu.SemaphoreType.DMA((len(ends),)),
        ],
        compiler_params=params(),
        name="cross_spectra",
    )(*blocks, whitened)


def local(spectra, source_index):
    ends, columns, column = edge_amplitudes(
        pltpu.with_memory_space_constraint(spectra, pltpu.HBM),
        pltpu.with_memory_space_constraint(source_index, pltpu.HBM),
    )
    row, total = extract_row(spectra, column)
    first = amplitudes(spectra, 0, row)
    return cross_spectra(*gather_rows(whiten_row(row, total, columns, first), spectra, first, ends))


def solution(mesh):
    def placed(spectra, source_index):
        with jax.sharding.use_abstract_mesh(mesh.abstract_mesh):
            return body(spectra, source_index)

    body = jax.shard_map(
        local,
        mesh=mesh,
        in_specs=(P(None, "band", None, "rx"), P()),
        out_specs=P(None, "band", None, "rx"),
        check_vma=False,
    )
    return placed
```
